512 devices in a mesh: band: 32 (over z, y_lo, core), row: 4 (over x), col: 4 (over y_hi).
Axes of the slice: x: 4, y: 8 (y_hi: 4, y_lo: 2; y = y_hi * 2 + y_lo), z: 8, core: 2. Of those that a mesh axis runs over, the one named last changes fastest.
Arguments:
- cond_orbitals: bfloat16 [512, 512000], P(('band', 'row', 'col')), may hold values from -6 to 6
- val_orbitals: bfloat16 [256, 512000], P(None, ('band', 'row', 'col')), may hold values from -6 to 6
- val_index: int32 [1], replicated, may hold values from 0 to 255
- val_energy: float32 [256], replicated, may hold values from -20 to -2
- cond_energy: float32 [512], replicated, may hold values from 1 to 40
- band_list: int32 [512], P(('band', 'row', 'col')), may hold values from 0 to 511, each once
- g_index: int32 [10240], replicated, may hold values from 0 to 511999, as said below
- chi_old: float32 [10240, 10240], P(('band', 'row'), 'col'), may hold values from -4 to 4
Outputs:
- chi_new: float32 [10240, 10240], P(('band', 'row'), 'col')
The draws below stay inside these ranges and needn't reach their ends.
Inputs may be any that keep to these rules, and one draw needn't show every extreme that they name: `g_index`: distinct flat grid indices (gx * 80 + gy) * 80 + gz of the 10240 frequencies nearest to zero, where a frequency above 40 counts as that frequency minus 80; equal distances in random order, listed by rising distance. `band_list`: each band number once.
All inputs are finite; a program needn't handle non-finite values.
Results may differ from the reference program's by a relative error of at most 0.013.
Values may be sent and summed in bfloat16 or wider, within the bound.
No kernel may reach another device: no remote copies, remote signals or barrier semaphores. Data moves between devices by JAX's collectives and lax.ppermute only.
A program may use at most 64 MiB of HBM per device.

```python
import math
import jax
import jax.numpy as jnp
from jax import lax

NS = 80
NG = 10240
NVAL = 256
NCOND = 512
GRID = 512000


def draw_g_index(key, part):
    key = jax.random.fold_in(key, 7)
    total = NS * NS * NS
    flat = jnp.arange(total, dtype=jnp.int32)
    freq_x = flat // (NS * NS)
    freq_y = flat // NS % NS
    freq_z = flat % NS
    signed_x = jnp.where(freq_x > NS // 2, freq_x - NS, freq_x)
    signed_y = jnp.where(freq_y > NS // 2, freq_y - NS, freq_y)
    signed_z = jnp.where(freq_z > NS // 2, freq_z - NS, freq_z)
    radius = signed_x * signed_x + signed_y * signed_y + signed_z * signed_z
    order = jax.random.permutation(key, total).astype(jnp.int32)
    shuffled = jnp.take(radius, order)
    ranking = jnp.argsort(shuffled, stable=True)
    return jnp.take(order, ranking[:NG]).astype(jnp.int32)


def block_scale(key, shape, cuts, smallest, top_value):
    loudness, own = 1.0, jax.random.fold_in(key, 6)
    for dim, parts in cuts:
        steps = jnp.exp(jax.random.uniform(jax.random.fold_in(own, dim), (parts,), jnp.float32, smallest / len(cuts), top_value / len(cuts)))
        loudness = loudness * jnp.repeat(steps, shape[dim] // parts).reshape([-1 if axis == dim else 1 for axis in range(len(shape))])
    return loudness


def gaussian(rng, dims, width, most, split=(), kind=jnp.bfloat16):
    loudness = block_scale(rng, dims, split, -0.22, 0.18) if split else 1.0
    entries = jax.random.normal(rng, dims, jnp.float32) * width * loudness
    return jnp.minimum(jnp.maximum(entries, -most), most).astype(kind)


def setup_inputs(seed: int = 0) -> dict:
    splits = jax.random.split(jax.random.key(seed), 9)
    return {
        "cond_orbitals": gaussian(splits[0], (NCOND, GRID), 1.0, 6.0, ((0, 512),)),
        "val_orbitals": gaussian(splits[1], (NVAL, GRID), 1.0, 6.0, ((1, 512),)),
        "val_index": jax.random.randint(splits[2], (1,), 0, NVAL).astype(jnp.int32),
        "val_energy": jnp.clip(jax.random.uniform(splits[3], (NVAL,), jnp.float32, -20.0, -2.0), -20.0, -2.0),
        "cond_energy": jnp.clip(jax.random.uniform(splits[4], (NCOND,), jnp.float32, 1.0, 40.0), 1.0, 40.0),
        "band_list": jax.random.permutation(splits[5], NCOND).astype(jnp.int32),
        "g_index": draw_g_index(jax.random.fold_in(splits[8], 71), 0),
        "chi_old": gaussian(splits[7], (NG, NG), 0.3, 4.0, ((0, 128), (1, 4)), jnp.float32),
    }


def cas_values(orbital, valence, g_index):
    product = valence.astype(jnp.float32) * orbital.astype(jnp.float32)
    density = lax.optimization_barrier(product.astype(jnp.bfloat16)).astype(jnp.float32)
    spectrum = jnp.fft.fftn(density.reshape(NS, NS, NS)).reshape(-1)
    picked = jnp.take(spectrum, g_index)
    cas = (jnp.real(picked) - jnp.imag(picked)) / math.sqrt(NS ** 3)
    return cas.astype(jnp.bfloat16)

def reference(cond_orbitals, val_orbitals, val_index, val_energy, cond_energy, band_list, g_index, chi_old):
    pick = val_index[0]
    valence = lax.dynamic_index_in_dim(val_orbitals, pick, 0, keepdims=False)
    e_val = lax.dynamic_index_in_dim(val_energy, pick, 0, keepdims=False)
    e_cond = jnp.take(cond_energy, band_list)
    weight = 4.0 / ((e_val - e_cond) * math.sqrt(NCOND))
    values = lax.map(lambda orbital: cas_values(orbital, valence, g_index), cond_orbitals)
    scaled = (weight[:, None] * values.astype(jnp.float32)).astype(jnp.bfloat16)
    update = jnp.dot(scaled.T, values, preferred_element_type=jnp.float32)
    return chi_old + update
```

```python
import math

import jax
import jax.numpy as jnp
import numpy as np
from jax import lax
from jax.experimental import pallas as pl
from jax.experimental.pallas import tpu as pltpu
from jax.sharding import Mesh, PartitionSpec as P

NS = 80
NG = 10240
NCOND = 512
GRID = NS**3
PIECE = 1000
KEPT = 14
BF16 = jnp.bfloat16
F32 = jnp.float32
AXES = ("za", "zb", "yl", "core", "x", "yh")
SIZES = (4, 2, 2, 2, 4, 4)
BAND = ("za", "zb", "yl", "core")
VMEM = pl.BlockSpec(memory_space=pltpu.VMEM)
SMEM = pl.BlockSpec(memory_space=pltpu.SMEM)


def tables():
    freq = np.arange(KEPT)
    angle = 2 * np.pi * np.outer(np.arange(NS), freq) / NS
    along_z = np.zeros((NS, 32))
    along_z[:, :KEPT] = np.cos(angle)
    along_z[:, 16 : 16 + KEPT] = np.sin(angle)
    first = np.kron(np.eye(8), along_z)
    row = np.arange(800)
    band = 2 * (row % 16) + row % 32 // 16
    line = 25 * band + row // 32
    angle = 2 * np.pi * np.outer(freq, line // 10) / NS
    along_x = np.zeros((32, 800))
    along_x[:KEPT] = np.cos(angle)
    along_x[16 : 16 + KEPT] = np.sin(angle)
    tens = line % 10
    along_q = np.concatenate(
        [
            np.cos(2 * np.pi * np.outer(np.arange(6), tens) / 10),
            np.sin(2 * np.pi * np.outer(np.arange(1, 5), tens) / 10),
        ]
    )
    second = (along_q[:, None, :] * along_x[None]).reshape(320, 800)
    angle = 2 * np.pi * np.outer(freq, np.arange(256) // 32) / NS
    third = np.zeros((32, 256))
    third[:KEPT] = np.cos(angle)
    third[16 : 16 + KEPT] = np.sin(angle)
    return first, second, third


def segments(m):
    found, lane = [], 0
    while lane < 128:
        piece, inside = divmod(128 * m + lane, PIECE)
        row, start = divmod(inside, 128)
        found.append((piece, row, lane))
        lane += min(128 - lane, 128 - start, PIECE - inside)
    return found


def index_parts(g_index):
    freq_z = g_index % NS
    freq_y = g_index // NS % NS
    freq_x = g_index // (NS * NS)

    def signed(freq):
        return jnp.where(freq > NS // 2, freq - NS, freq)

    x, y, z = signed(freq_x), signed(freq_y), signed(freq_z)
    sign = (x < 0).astype(jnp.int32) + 2 * (y < 0) + 4 * (z < 0)
    high = (jnp.abs(y) // 2) * 16 + jnp.abs(x)
    low = (jnp.abs(y) % 2) * 128 + sign * 16 + jnp.abs(z)
    return low, high


def values_kernel(
    pick_ref, energy_ref, own_ref, other_ref, cond_ref, low_ref, high_ref, bands_ref,
    first_ref, second_ref, third_ref, h_ref, weight_ref, val, block, rows,
):
    core = lax.axis_index("core")
    half = own_ref.shape[0]
    start = pl.multiple_of(core * half, half)
    val[pl.ds(start, half), :] = own_ref[...].astype(F32)
    val[pl.ds(pl.multiple_of(half - start, half), half), :] = other_ref[...].astype(F32)

    inside = (lax.axis_index("zb") * 2 + lax.axis_index("yl")) * 128 + lax.axis_index("x") * 32 + 7
    lane = lax.broadcasted_iota(jnp.int32, (16, 128), 1)
    tail = jnp.concatenate(
        [
            val[pl.ds(start + inside + 512 * za + 8 * yh, 1), :]
            for za in range(4)
            for yh in range(4)
        ],
        axis=0,
    )
    upper = jnp.sum(jnp.where(lane == 104, tail, 0.0), axis=1, keepdims=True)
    lower = jnp.sum(jnp.where(lane == 105, tail, 0.0), axis=1, keepdims=True)
    number = (2.0 * upper + lower).astype(jnp.int32)
    match = lax.broadcasted_iota(jnp.int32, (16, NCOND), 1) == number
    e_cond = jnp.sum(jnp.where(match, bands_ref[...], 0.0), axis=1, keepdims=True)
    e_val = energy_ref[pick_ref[0]]
    weight = 4.0 / ((e_val - e_cond) * math.sqrt(NCOND))
    weight_ref[...] = jnp.broadcast_to(weight, (16, 128))

    lane = lax.broadcasted_iota(jnp.int32, (32, 128), 1)
    turned = {}

    def turn(piece, row):
        if (piece, row) not in turned:
            found = val[pl.ds(8 * piece + row, 32, stride=128), :]
            shift = 104 * piece % 128
            turned[piece, row] = pltpu.roll(found, shift, 1) if shift else found
        return turned[piece, row]

    parts = []
    for n in range(25):
        for t in range(5):
            m = 5 * n + t
            valence = None
            for piece, row, begin in segments(m):
                found = turn(piece, row)
                valence = found if valence is None else jnp.where(lane >= begin, found, valence)
            orbital = jnp.concatenate(
                [cond_ref[pl.ds(m + 125 * c, 16, stride=250), :] for c in range(2)], axis=0
            )
            block[32 * n : 32 * n + 32, 128 * t : 128 * t + 128] = (valence * orbital).astype(BF16)
        if n % 5 == 4:
            parts.append(
                jnp.dot(
                    block[32 * (n - 4) : 32 * (n + 1), :],
                    first_ref[...],
                    preferred_element_type=F32,
                ).astype(BF16)
            )
    second = jnp.dot(second_ref[...], jnp.concatenate(parts, axis=0), preferred_element_type=F32)

    lane = lax.broadcasted_iota(jnp.int32, (16, 128), 1)
    group = lane // 16
    even = group % 2 == 0
    sx = jnp.where(group & 1 == 0, 1.0, -1.0)
    sy = jnp.where(group & 2 == 0, 1.0, -1.0)
    sz = jnp.where(group & 4 == 0, 1.0, -1.0)
    sxy, sxz, syz = sx * sy, sx * sz, sy * sz
    sxyz = sxy * sz

    def add_lanes(value):
        value = value[:, :128] + value[:, 128:]
        value = value + pltpu.roll(value, 64, 1)
        return value + pltpu.roll(value, 32, 1)

    def split(value):
        other = pltpu.roll(value, 16, 1)
        found = []
        for begin in (0, 16):
            a, b = value[begin : begin + 16], other[begin : begin + 16]
            found += [jnp.where(even, a, b), jnp.where(even, b, a)]
        return found

    planes = []
    for gy in range(KEPT):
        digit, sign = gy % 10, 1.0
        if digit > 5:
            digit, sign = 10 - digit, -1.0
        cosine, sine = third_ref[gy : gy + 1, :], third_ref[16 + gy : 17 + gy, :]
        even_q = second[32 * digit : 32 * digit + 32]
        re, im = even_q * cosine, even_q * sine
        if 1 <= digit <= 4:
            odd_q = second[32 * (digit + 5) : 32 * (digit + 5) + 32]
            re, im = re - (sign * sine) * odd_q, im + (sign * cosine) * odd_q
        ccc, ccs, scc, scs = split(add_lanes(re))
        csc, css, ssc, sss = split(add_lanes(im))
        total = (
            (ccc - syz * css) + (sz * ccs + sy * csc) + (sx * scc - sxz * scs) - (sxy * ssc + sxyz * sss)
        )
        planes.append((total * (1.0 / math.sqrt(GRID))).astype(BF16))
    cube = jnp.concatenate(
        [jnp.concatenate(planes[2 * i : 2 * i + 2], axis=1) for i in range(7)], axis=0
    )

    width = 1280
    place = lax.broadcasted_iota(jnp.int32, (112, width), 0)
    inner = lax.broadcasted_iota(jnp.int32, (256, width), 0)
    for c in range(NG // width):
        part = slice(c * width, (c + 1) * width)
        chosen = jnp.where(inner == low_ref[:, part], 1.0, 0.0).astype(BF16)
        found = jnp.dot(cube, chosen, preferred_element_type=F32)
        found = jnp.sum(jnp.where(place == high_ref[:, part], found, 0.0), axis=0, keepdims=True)
        for k in range(width // 128):
            rows[c * (width // 128) + k : c * (width // 128) + k + 1, :] = found[:, 128 * k : 128 * k + 128]
    mine = rows[...].astype(BF16)
    for k in range(16):
        h_ref[k] = mine


def pack_kernel(h_ref, weight_ref, out_ref, wide, full):
    wide[...] = h_ref[...].reshape(16 * 80, 128).astype(F32)
    for k in range(80):
        full[:, 128 * k : 128 * k + 128] = wide[pl.ds(k, 16, stride=80), :]
    col = lax.axis_index("yh") * 2560
    for c in range(2):
        cols = full[:, pl.ds(pl.multiple_of(col + 1280 * c, 128), 1280)].astype(BF16)
        for k in range(32):
            if k // 4 % 2 == c:
                out_ref[k, :, 0:1280] = cols
    rows = full[:, pl.ds(pl.multiple_of(lax.axis_index("za") * 2560, 128), 2560)]
    rows = weight_ref[:, 0:1] * rows
    for k in range(32):
        for at, piece in ((1280, k), (1408, k ^ 4)):
            begin = 80 * piece
            first, shift = begin // 128 * 128, begin % 128
            found = rows[:, first : first + 128]
            if shift:
                found = pltpu.roll(found, 128 - shift, 1)
                if shift > 48:
                    after = pltpu.roll(rows[:, first + 128 : first + 256], 128 - shift, 1)
                    lane = lax.broadcasted_iota(jnp.int32, (16, 128), 1)
                    found = jnp.where(lane < 128 - shift, found, after)
            out_ref[k, :, at : at + 128] = found.astype(BF16)


def product_kernel(begin, all_ref, out_ref):
    left = all_ref[:, begin : begin + 128]
    out_ref[...] = lax.dot_general(
        left, all_ref[:, 0:1280], (((0,), (0,)), ((), ())), preferred_element_type=F32
    )[0:80]


def finish_kernel(chi_ref, own_ref, other_ref, out_ref):
    core = lax.axis_index("core")
    at = pl.multiple_of(core * 1280, 1280)
    off = pl.multiple_of(1280 - core * 1280, 1280)
    out_ref[:, pl.ds(at, 1280)] = chi_ref[:, pl.ds(at, 1280)] + own_ref[...]
    out_ref[:, pl.ds(off, 1280)] = chi_ref[:, pl.ds(off, 1280)] + other_ref[...]


def call(kernel, out, in_specs, scratch=(), mib=16, flops=0, moved=0):
    return pl.pallas_call(
        kernel,
        out_shape=out,
        in_specs=in_specs,
        out_specs=jax.tree.map(lambda _: VMEM, out),
        scratch_shapes=scratch,
        compiler_params=pltpu.CompilerParams(vmem_limit_bytes=mib * 2**20),
        cost_estimate=pl.CostEstimate(flops=flops, bytes_accessed=moved, transcendentals=0),
    )


def body(cond_orbitals, val_orbitals, val_index, val_energy, cond_energy, band_list, g_index, chi_old):
    shape = jax.ShapeDtypeStruct
    pick = val_index[0]
    piece = lax.dynamic_index_in_dim(val_orbitals, pick, 0, keepdims=False)
    tail = jnp.concatenate([band_list // 2, band_list % 2]).astype(BF16)
    piece = jnp.concatenate([piece, tail, jnp.zeros((22,), BF16)]).reshape(1, 8, 128)
    own = lax.all_to_all(
        jnp.broadcast_to(piece, (256, 8, 128)), ("za", "zb", "yl", "x", "yh"), 0, 0, tiled=True
    ).reshape(2048, 128)
    other = lax.ppermute(own, "core", [(0, 1), (1, 0)])
    orbital = cond_orbitals.astype(F32).reshape(4000, 128)
    low, high = index_parts(g_index)
    first, second, third = tables()
    values, weight = call(
        values_kernel,
        (shape((16, 80, 128), BF16), shape((16, 128), F32)),
        [SMEM, SMEM] + [VMEM] * 9,
        [pltpu.VMEM((4096, 128), F32), pltpu.VMEM((800, 640), BF16), pltpu.VMEM((80, 128), F32)],
        mib=32,
    )(
        val_index, val_energy, own, other, orbital, low.reshape(1, NG), high.reshape(1, NG),
        cond_energy.reshape(1, NCOND), jnp.asarray(first, BF16), jnp.asarray(second, BF16), jnp.asarray(third, F32),
    )
    gathered = lax.all_to_all(values, ("za", "yh"), 0, 0, tiled=True)
    packed = call(
        pack_kernel,
        shape((32, 16, 1536), BF16),
        [VMEM] * 2,
        [pltpu.VMEM((1280, 128), F32), pltpu.VMEM((16, NG), F32)],
    )(gathered, weight)
    panel = lax.all_to_all(packed, ("zb", "yl", "core", "x"), 0, 0, tiled=True).reshape(512, 1536)
    block = shape((80, 1280), F32)
    given = call(lambda *refs: product_kernel(1408, *refs), block, [VMEM])(panel)
    taken = lax.ppermute(given, "core", [(0, 1), (1, 0)])
    kept = call(lambda *refs: product_kernel(1280, *refs), block, [VMEM])(panel)
    return call(finish_kernel, shape((80, 2560), F32), [VMEM] * 3)(chi_old, kept, taken)


def solution(mesh):
    fine = Mesh(mesh.devices.reshape(SIZES), AXES)
    every = AXES
    return jax.shard_map(
        body,
        mesh=fine,
        in_specs=(
            P(every, None),
            P(None, every),
            P(),
            P(),
            P(),
            P(every),
            P(),
            P(BAND + ("x",), "yh"),
        ),
        out_specs=P(BAND + ("x",), "yh"),
        check_vma=False,
    )
```

```python
import math

import jax
import jax.numpy as jnp
import numpy as np
from jax import lax
from jax.experimental import pallas as pl
from jax.experimental.pallas import tpu as pltpu
from jax.sharding import Mesh, PartitionSpec as P

NS = 80
NG = 10240
NCOND = 512
GRID = NS**3
PIECE = 1000
KEPT = 14
BF16 = jnp.bfloat16
F32 = jnp.float32
AXES = ("za", "zb", "yl", "core", "x", "yh")
SIZES = (4, 2, 2, 2, 4, 4)
BAND = ("za", "zb", "yl", "core")
VMEM = pl.BlockSpec(memory_space=pltpu.VMEM)
SMEM = pl.BlockSpec(memory_space=pltpu.SMEM)


def tables():
    freq = np.arange(KEPT)
    angle = 2 * np.pi * np.outer(np.arange(NS), freq) / NS
    along_z = np.zeros((NS, 32))
    along_z[:, :KEPT] = np.cos(angle)
    along_z[:, 16 : 16 + KEPT] = np.sin(angle)
    first = np.kron(np.eye(8), along_z)
    row = np.arange(800)
    band = 2 * (row % 16) + row % 32 // 16
    line = 25 * band + row // 32
    angle = 2 * np.pi * np.outer(freq, line // 10) / NS
    along_x = np.zeros((32, 800))
    along_x[:KEPT] = np.cos(angle)
    along_x[16 : 16 + KEPT] = np.sin(angle)
    tens = line % 10
    along_q = np.concatenate(
        [
            np.cos(2 * np.pi * np.outer(np.arange(6), tens) / 10),
            np.sin(2 * np.pi * np.outer(np.arange(1, 5), tens) / 10),
        ]
    )
    second = (along_q[:, None, :] * along_x[None]).reshape(320, 800)
    angle = 2 * np.pi * np.outer(freq, np.arange(256) // 32) / NS
    third = np.zeros((32, 256))
    third[:KEPT] = np.cos(angle)
    third[16 : 16 + KEPT] = np.sin(angle)
    return first, second, third


def segments(m):
    found, lane = [], 0
    while lane < 128:
        piece, inside = divmod(128 * m + lane, PIECE)
        row, start = divmod(inside, 128)
        found.append((piece, row, lane))
        lane += min(128 - lane, 128 - start, PIECE - inside)
    return found


def index_parts(g_index):
    freq_z = g_index % NS
    freq_y = g_index // NS % NS
    freq_x = g_index // (NS * NS)

    def signed(freq):
        return jnp.where(freq > NS // 2, freq - NS, freq)

    x, y, z = signed(freq_x), signed(freq_y), signed(freq_z)
    sign = (x < 0).astype(jnp.int32) + 2 * (y < 0) + 4 * (z < 0)
    high = (jnp.abs(y) // 2) * 16 + jnp.abs(x)
    low = (jnp.abs(y) % 2) * 128 + sign * 16 + jnp.abs(z)
    return low, high


def values_kernel(
    pick_ref, number_ref, val_energy_ref, cond_energy_ref, own_ref, other_ref, cond_ref, chosen_ref, high_ref,
    first_ref, second_ref, third_ref, out_ref, val, block, rows, scaled, points, arrived,
):
    fetch = pltpu.make_async_copy(chosen_ref, points, arrived)
    fetch.start()
    core = lax.axis_index("core")
    half = own_ref.shape[0]
    start = pl.multiple_of(core * half, half)
    val[pl.ds(start, half), :] = own_ref[...].astype(F32)
    val[pl.ds(pl.multiple_of(half - start, half), half), :] = other_ref[...].astype(F32)
    e_val = jnp.full((1, 128), val_energy_ref[pick_ref[0]], F32)
    e_cond = jnp.full((1, 128), cond_energy_ref[number_ref[0]], F32)
    weight = 4.0 / ((e_val - e_cond) * math.sqrt(NCOND))

    lane = lax.broadcasted_iota(jnp.int32, (32, 128), 1)
    turned = {}

    def turn(piece, row):
        if (piece, row) not in turned:
            at = piece // 4 * 512 + piece % 4 * 8 + row
            found = jnp.concatenate(
                [val[pl.ds(at + half * c, 16, stride=32), :] for c in range(2)], axis=0
            )
            shift = 104 * piece % 128
            turned[piece, row] = pltpu.roll(found, shift, 1) if shift else found
        return turned[piece, row]

    parts = []
    for n in range(25):
        for t in range(5):
            m = 5 * n + t
            valence = None
            for piece, row, begin in segments(m):
                found = turn(piece, row)
                valence = found if valence is None else jnp.where(lane >= begin, found, valence)
            orbital = jnp.concatenate(
                [cond_ref[pl.ds(m + 125 * c, 16, stride=250), :] for c in range(2)], axis=0
            )
            block[32 * n : 32 * n + 32, 128 * t : 128 * t + 128] = (valence * orbital).astype(BF16)
        if n % 5 == 4:
            parts.append(
                jnp.dot(
                    block[32 * (n - 4) : 32 * (n + 1), :],
                    first_ref[...],
                    preferred_element_type=F32,
                ).astype(BF16)
            )
    second = jnp.dot(second_ref[...], jnp.concatenate(parts, axis=0), preferred_element_type=F32)

    lane = lax.broadcasted_iota(jnp.int32, (16, 128), 1)
    group = lane // 16
    even = group % 2 == 0
    sx = jnp.where(group & 1 == 0, 1.0, -1.0)
    sy = jnp.where(group & 2 == 0, 1.0, -1.0)
    sz = jnp.where(group & 4 == 0, 1.0, -1.0)
    sxy, sxz, syz = sx * sy, sx * sz, sy * sz
    sxyz = sxy * sz

    def add_lanes(value):
        value = value[:, :128] + value[:, 128:]
        value = value + pltpu.roll(value, 64, 1)
        return value + pltpu.roll(value, 32, 1)

    def split(value):
        other = pltpu.roll(value, 16, 1)
        found = []
        for begin in (0, 16):
            a, b = value[begin : begin + 16], other[begin : begin + 16]
            found += [jnp.where(even, a, b), jnp.where(even, b, a)]
        return found

    planes = []
    for gy in range(KEPT):
        digit, sign = gy % 10, 1.0
        if digit > 5:
            digit, sign = 10 - digit, -1.0
        cosine, sine = third_ref[gy : gy + 1, :], third_ref[16 + gy : 17 + gy, :]
        even_q = second[32 * digit : 32 * digit + 32]
        re, im = even_q * cosine, even_q * sine
        if 1 <= digit <= 4:
            odd_q = second[32 * (digit + 5) : 32 * (digit + 5) + 32]
            re, im = re - (sign * sine) * odd_q, im + (sign * cosine) * odd_q
        ccc, ccs, scc, scs = split(add_lanes(re))
        csc, css, ssc, sss = split(add_lanes(im))
        total = (
            (ccc - syz * css) + (sz * ccs + sy * csc) + (sx * scc - sxz * scs) - (sxy * ssc + sxyz * sss)
        )
        planes.append((total * (1.0 / math.sqrt(GRID))).astype(BF16))
    cube = jnp.concatenate(
        [jnp.concatenate(planes[2 * i : 2 * i + 2], axis=1) for i in range(7)], axis=0
    )

    width = 1280
    place = lax.broadcasted_iota(jnp.int32, (112, width), 0)
    fetch.wait()
    for c in range(NG // width):
        part = slice(c * width, (c + 1) * width)
        found = jnp.dot(cube, points[:, part], preferred_element_type=F32)
        found = jnp.sum(jnp.where(place == high_ref[:, part], found, 0.0), axis=0, keepdims=True)
        found = found.astype(BF16).astype(F32)
        for k in range(width // 128):
            at = c * (width // 128) + k
            piece = found[:, 128 * k : 128 * k + 128]
            rows[at : at + 1, :] = piece
            scaled[at : at + 1, :] = weight * piece
    for k in range(16):
        yh, za = k % 4, k // 4
        out_ref[k] = jnp.concatenate(
            [rows[20 * yh : 20 * yh + 20, :], scaled[20 * za : 20 * za + 20, :]], axis=0
        ).astype(BF16)


def chosen_kernel(low_ref, out_ref):
    width = 1280
    inner = lax.broadcasted_iota(jnp.int32, (256, width), 0)
    for c in range(NG // width):
        part = slice(c * width, (c + 1) * width)
        out_ref[:, part] = jnp.where(inner == low_ref[:, part], 1.0, 0.0).astype(BF16)


def pack_kernel(h_ref, out_ref, wide, full):
    wide[...] = h_ref[...].reshape(16 * 40, 128).astype(F32)
    for k in range(40):
        full[:, 128 * k : 128 * k + 128] = wide[pl.ds(k, 16, stride=40), :]
    cols = full[:, 0:2560].astype(BF16)
    lane = lax.broadcasted_iota(jnp.int32, (16, 128), 1)
    core = lax.axis_index("core")
    for k in range(16):
        out_ref[k, :, 0:2560] = cols
        pieces = []
        for c in range(2):
            begin = 80 * (k // 4 * 8 + 4 * c + k % 4)
            first, shift = 2560 + begin // 128 * 128, begin % 128
            found = full[:, first : first + 128]
            if shift:
                found = pltpu.roll(found, 128 - shift, 1)
                if shift > 48:
                    after = pltpu.roll(full[:, first + 128 : first + 256], 128 - shift, 1)
                    found = jnp.where(lane < 128 - shift, found, after)
            pieces.append(found)
        mine = jnp.where(core == 0, pieces[0], pieces[1])
        theirs = jnp.where(core == 0, pieces[1], pieces[0])
        out_ref[k, :, 2560:2688] = mine.astype(BF16)
        out_ref[k, :, 2688:2816] = theirs.astype(BF16)


def times(left, right):
    return lax.dot_general(left, right, (((0,), (0,)), ((), ())), preferred_element_type=F32)[0:80]


def given_kernel(all_ref, out_ref):
    out_ref[...] = times(all_ref[:, 2688:2816], all_ref[:, 0:2560])


def kept_kernel(all_ref, chi_ref, out_ref):
    out_ref[...] = chi_ref[...] + times(all_ref[:, 2560:2688], all_ref[:, 0:2560])


def finish_kernel(kept_ref, taken_ref, out_ref):
    out_ref[...] = kept_ref[...] + taken_ref[...]


def call(kernel, out, in_specs, scratch=(), mib=16, flops=0, moved=0):
    return pl.pallas_call(
        kernel,
        out_shape=out,
        in_specs=in_specs,
        out_specs=jax.tree.map(lambda _: VMEM, out),
        scratch_shapes=scratch,
        compiler_params=pltpu.CompilerParams(vmem_limit_bytes=mib * 2**20),
        cost_estimate=pl.CostEstimate(flops=flops, bytes_accessed=moved, transcendentals=0),
    )


def body(cond_orbitals, val_orbitals, val_index, val_energy, cond_energy, band_list, g_index, chi_old):
    shape = jax.ShapeDtypeStruct
    piece = lax.dynamic_index_in_dim(val_orbitals, val_index[0], 0, keepdims=False)
    piece = jnp.pad(piece, (0, 24)).reshape(1, 8, 128)
    own = lax.all_to_all(
        jnp.broadcast_to(piece, (64, 8, 128)), ("za", "zb", "yl", "yh"), 0, 0, tiled=True
    )
    orbital = cond_orbitals.astype(F32).reshape(4000, 128)
    low, high = index_parts(g_index)
    chosen = call(chosen_kernel, shape((256, NG), BF16), [VMEM], moved=2**23)(low.reshape(1, NG))
    chosen = pltpu.with_memory_space_constraint(chosen, pltpu.HBM)
    own, orbital, chosen, high = lax.optimization_barrier((own, orbital, chosen, high))
    own = lax.all_to_all(
        jnp.broadcast_to(own.reshape(1, 512, 128), (4, 512, 128)), "x", 0, 0, tiled=True
    ).reshape(2048, 128)
    other = lax.ppermute(own, "core", [(0, 1), (1, 0)])
    first, second, third = tables()
    values = call(
        values_kernel,
        shape((16, 40, 128), BF16),
        [SMEM] * 4 + [VMEM] * 3 + [pl.BlockSpec(memory_space=pltpu.HBM)] + [VMEM] * 4,
        [pltpu.VMEM((4096, 128), F32), pltpu.VMEM((800, 640), BF16)]
        + [pltpu.VMEM((80, 128), F32)] * 2
        + [pltpu.VMEM((256, NG), BF16), pltpu.SemaphoreType.DMA(())],
        mib=24,
    )(
        val_index, band_list, val_energy, cond_energy, own, other, orbital, chosen, high.reshape(1, NG),
        jnp.asarray(first, BF16), jnp.asarray(second, BF16), jnp.asarray(third, F32),
    )
    gathered = lax.all_to_all(values, ("za", "yh"), 0, 0, tiled=True)
    packed = call(
        pack_kernel,
        shape((16, 16, 2816), BF16),
        [VMEM],
        [pltpu.VMEM((640, 128), F32), pltpu.VMEM((16, 5120), F32)],
    )(gathered)
    panel = lax.all_to_all(packed, ("zb", "yl", "x"), 0, 0, tiled=True).reshape(256, 2816)
    block = shape((80, 2560), F32)
    given = call(given_kernel, block, [VMEM])(panel)
    taken = lax.ppermute(given, "core", [(0, 1), (1, 0)])
    kept = call(kept_kernel, block, [VMEM] * 2)(panel, chi_old)
    return call(finish_kernel, block, [VMEM] * 2)(kept, taken)


def solution(mesh):
    fine = Mesh(mesh.devices.reshape(SIZES), AXES)
    every = AXES
    return jax.shard_map(
        body,
        mesh=fine,
        in_specs=(
            P(every, None),
            P(None, every),
            P(),
            P(),
            P(),
            P(every),
            P(),
            P(BAND + ("x",), "yh"),
        ),
        out_specs=P(BAND + ("x",), "yh"),
        check_vma=False,
    )
```

```python
import math

import jax
import jax.numpy as jnp
import numpy as np
from jax import lax
from jax.experimental import pallas as pl
from jax.experimental.pallas import tpu as pltpu
from jax.sharding import Mesh, PartitionSpec as P

NS = 80
NG = 10240
NCOND = 512
GRID = NS**3
PIECE = 1000
KEPT = 14
BF16 = jnp.bfloat16
F32 = jnp.float32
AXES = ("za", "zb", "yl", "core", "x", "yh")
SIZES = (4, 2, 2, 2, 4, 4)
BAND = ("za", "zb", "yl", "core")
VMEM = pl.BlockSpec(memory_space=pltpu.VMEM)
SMEM = pl.BlockSpec(memory_space=pltpu.SMEM)


def tables():
    freq = np.arange(KEPT)
    angle = 2 * np.pi * np.outer(np.arange(NS), freq) / NS
    along_z = np.zeros((NS, 32))
    along_z[:, :KEPT] = np.cos(angle)
    along_z[:, 16 : 16 + KEPT] = np.sin(angle)
    first = np.kron(np.eye(8), along_z)
    core, row = np.divmod(np.arange(800), 400)
    line = 25 * (2 * (row % 16) + core) + row // 16
    angle = 2 * np.pi * np.outer(freq, line // 10) / NS
    along_x = np.zeros((32, 800))
    along_x[:KEPT] = np.cos(angle)
    along_x[16 : 16 + KEPT] = np.sin(angle)
    tens = line % 10
    along_q = np.concatenate(
        [
            np.cos(2 * np.pi * np.outer(np.arange(6), tens) / 10),
            np.sin(2 * np.pi * np.outer(np.arange(1, 5), tens) / 10),
        ]
    )
    second = (along_q[:, None, :] * along_x[None]).reshape(320, 2, 400).transpose(1, 0, 2)
    angle = 2 * np.pi * np.outer(freq, np.arange(256) // 32) / NS
    third = np.zeros((32, 256))
    third[:KEPT] = np.cos(angle)
    third[16 : 16 + KEPT] = np.sin(angle)
    return first, second, third


def segments(m):
    found, lane = [], 0
    while lane < 128:
        piece, inside = divmod(128 * m + lane, PIECE)
        row, start = divmod(inside, 128)
        found.append((piece, row, lane))
        lane += min(128 - lane, 128 - start, PIECE - inside)
    return found


def index_parts(g_index):
    freq_z = g_index % NS
    freq_y = g_index // NS % NS
    freq_x = g_index // (NS * NS)

    def signed(freq):
        return jnp.where(freq > NS // 2, freq - NS, freq)

    x, y, z = signed(freq_x), signed(freq_y), signed(freq_z)
    sign = (x < 0).astype(jnp.int32) + 2 * (y < 0) + 4 * (z < 0)
    high = (jnp.abs(y) // 2) * 16 + jnp.abs(x)
    low = (jnp.abs(y) % 2) * 128 + sign * 16 + jnp.abs(z)
    return low, high


def pick_kernel(pick_ref, val_ref, out_ref, line):
    chosen = lax.broadcasted_iota(jnp.int32, (8, 256), 1) == pick_ref[0]
    line[...] = jnp.zeros(line.shape, F32)
    line[:, 0:PIECE] = lax.dot_general(
        jnp.where(chosen, 1.0, 0.0).astype(BF16), val_ref[...], (((1,), (1,)), ((), ())), preferred_element_type=F32
    )
    row = lax.broadcasted_iota(jnp.int32, (8, 128), 0)
    piece = line[:, 0:128]
    for k in range(1, 8):
        piece = jnp.where(row == k, line[:, 128 * k : 128 * k + 128], piece)
    piece = piece.astype(BF16)
    for k in range(64):
        out_ref[k] = piece


def half_grid(core, valence_ref, cond_ref, first_ref, second_ref, val, block):
    val[...] = valence_ref[...].astype(F32)
    lane = lax.broadcasted_iota(jnp.int32, (16, 128), 1)
    turned = {}

    def turn(piece, row):
        if (piece, row) not in turned:
            at = piece // 4 * 512 + piece % 4 * 8 + row
            found = val[pl.ds(at, 16, stride=32), :]
            shift = 104 * piece % 128
            turned[piece, row] = pltpu.roll(found, shift, 1) if shift else found
        return turned[piece, row]

    parts = []
    for n in range(25):
        for t in range(5):
            m = 5 * n + t
            valence = None
            for piece, row, begin in segments(m):
                found = turn(piece, row)
                valence = found if valence is None else jnp.where(lane >= begin, found, valence)
            orbital = cond_ref[pl.ds(m + 125 * core, 16, stride=250), :]
            block[16 * n : 16 * n + 16, 128 * t : 128 * t + 128] = (valence * orbital).astype(BF16)
        if n % 5 == 4:
            parts.append(
                jnp.dot(
                    block[16 * (n - 4) : 16 * (n + 1), :],
                    first_ref[...],
                    preferred_element_type=F32,
                ).astype(BF16)
            )
    return jnp.dot(second_ref[core], jnp.concatenate(parts, axis=0), preferred_element_type=F32)


def own_kernel(own_ref, cond_ref, first_ref, second_ref, out_ref, val, block):
    core = lax.axis_index("core")
    out_ref[...] = half_grid(core, own_ref, cond_ref, first_ref, second_ref, val, block)


def values_kernel(
    pick_ref, number_ref, val_energy_ref, cond_energy_ref, half_ref, other_ref, cond_ref, chosen_ref, high_ref,
    first_ref, second_ref, third_ref, out_ref, val, block, rows, scaled,
):
    e_val = jnp.full((1, 128), val_energy_ref[pick_ref[0]], F32)
    e_cond = jnp.full((1, 128), cond_energy_ref[number_ref[0]], F32)
    weight = 4.0 / ((e_val - e_cond) * math.sqrt(NCOND))
    core = 1 - lax.axis_index("core")
    second = half_ref[...] + half_grid(core, other_ref, cond_ref, first_ref, second_ref, val, block)

    lane = lax.broadcasted_iota(jnp.int32, (16, 128), 1)
    group = lane // 16
    even = group % 2 == 0
    sx = jnp.where(group & 1 == 0, 1.0, -1.0)
    sy = jnp.where(group & 2 == 0, 1.0, -1.0)
    sz = jnp.where(group & 4 == 0, 1.0, -1.0)
    sxy, sxz, syz = sx * sy, sx * sz, sy * sz
    sxyz = sxy * sz

    def add_lanes(value):
        value = value[:, :128] + value[:, 128:]
        value = value + pltpu.roll(value, 64, 1)
        return value + pltpu.roll(value, 32, 1)

    def split(value):
        other = pltpu.roll(value, 16, 1)
        found = []
        for begin in (0, 16):
            a, b = value[begin : begin + 16], other[begin : begin + 16]
            found += [jnp.where(even, a, b), jnp.where(even, b, a)]
        return found

    planes = []
    for gy in range(KEPT):
        digit, sign = gy % 10, 1.0
        if digit > 5:
            digit, sign = 10 - digit, -1.0
        cosine, sine = third_ref[gy : gy + 1, :], third_ref[16 + gy : 17 + gy, :]
        even_q = second[32 * digit : 32 * digit + 32]
        re, im = even_q * cosine, even_q * sine
        if 1 <= digit <= 4:
            odd_q = second[32 * (digit + 5) : 32 * (digit + 5) + 32]
            re, im = re - (sign * sine) * odd_q, im + (sign * cosine) * odd_q
        ccc, ccs, scc, scs = split(add_lanes(re))
        csc, css, ssc, sss = split(add_lanes(im))
        total = (
            (ccc - syz * css) + (sz * ccs + sy * csc) + (sx * scc - sxz * scs) - (sxy * ssc + sxyz * sss)
        )
        planes.append((total * (1.0 / math.sqrt(GRID))).astype(BF16))
    cube = jnp.concatenate(
        [jnp.concatenate(planes[2 * i : 2 * i + 2], axis=1) for i in range(7)], axis=0
    )

    width = 1280
    place = lax.broadcasted_iota(jnp.int32, (112, width), 0)
    for c in range(NG // width):
        part = slice(c * width, (c + 1) * width)
        found = jnp.dot(cube, chosen_ref[:, part], preferred_element_type=F32)
        found = jnp.sum(jnp.where(place == high_ref[:, part], found, 0.0), axis=0, keepdims=True)
        found = found.astype(BF16).astype(F32)
        for k in range(width // 128):
            at = c * (width // 128) + k
            piece = found[:, 128 * k : 128 * k + 128]
            rows[at : at + 1, :] = piece
            scaled[at : at + 1, :] = weight * piece
    for k in range(16):
        yh, za = k % 4, k // 4
        out_ref[k] = jnp.concatenate(
            [rows[20 * yh : 20 * yh + 20, :], scaled[20 * za : 20 * za + 20, :]], axis=0
        ).astype(BF16)


def chosen_kernel(low_ref, out_ref, done_ref):
    width = 1280
    done_ref[...] = jnp.zeros((8, 128), F32)
    inner = lax.broadcasted_iota(jnp.int32, (256, width), 0)
    for c in range(NG // width):
        part = slice(c * width, (c + 1) * width)
        out_ref[:, part] = jnp.where(inner == low_ref[:, part], 1.0, 0.0).astype(BF16)


def spread_kernel(own_ref, done_ref, out_ref):
    for k in range(4):
        out_ref[k] = own_ref[...]


def pack_kernel(h_ref, out_ref, wide, full):
    wide[...] = h_ref[...].reshape(16 * 40, 128).astype(F32)
    for k in range(40):
        full[:, 128 * k : 128 * k + 128] = wide[pl.ds(k, 16, stride=40), :]
    cols = full[:, 0:2560].astype(BF16)
    lane = lax.broadcasted_iota(jnp.int32, (16, 128), 1)
    core = lax.axis_index("core")
    for k in range(16):
        out_ref[k, :, 0:2560] = cols
        pieces = []
        for c in range(2):
            begin = 80 * (k // 4 * 8 + 4 * c + k % 4)
            first, shift = 2560 + begin // 128 * 128, begin % 128
            found = full[:, first : first + 128]
            if shift:
                found = pltpu.roll(found, 128 - shift, 1)
                if shift > 48:
                    after = pltpu.roll(full[:, first + 128 : first + 256], 128 - shift, 1)
                    found = jnp.where(lane < 128 - shift, found, after)
            pieces.append(found)
        mine = jnp.where(core == 0, pieces[0], pieces[1])
        theirs = jnp.where(core == 0, pieces[1], pieces[0])
        out_ref[k, :, 2560:2688] = mine.astype(BF16)
        out_ref[k, :, 2688:2816] = theirs.astype(BF16)


def times(left, right):
    return lax.dot_general(left, right, (((0,), (0,)), ((), ())), preferred_element_type=F32)[0:80]


def given_kernel(all_ref, out_ref):
    out_ref[...] = times(all_ref[:, 2688:2816], all_ref[:, 0:2560])


def kept_kernel(all_ref, chi_ref, out_ref):
    out_ref[...] = chi_ref[...] + times(all_ref[:, 2560:2688], all_ref[:, 0:2560])


def finish_kernel(kept_ref, taken_ref, out_ref, total, sent):
    copies = []
    for k in range(5):
        part = pl.ds(16 * k, 16)
        total[part, :] = kept_ref[part, :] + taken_ref[part, :]
        copies.append(pltpu.make_async_copy(total.at[part], out_ref.at[part], sent.at[k]))
        copies[-1].start()
    for copy in copies:
        copy.wait()


def call(kernel, out, in_specs, scratch=(), mib=16, flops=0, moved=0, where=VMEM):
    return pl.pallas_call(
        kernel,
        out_shape=out,
        in_specs=in_specs,
        out_specs=jax.tree.map(lambda _: where, out),
        scratch_shapes=scratch,
        compiler_params=pltpu.CompilerParams(vmem_limit_bytes=mib * 2**20),
        cost_estimate=pl.CostEstimate(flops=flops, bytes_accessed=moved, transcendentals=0),
    )


def body(cond_orbitals, val_orbitals, val_index, val_energy, cond_energy, band_list, g_index, chi_old):
    shape = jax.ShapeDtypeStruct
    piece = call(pick_kernel, shape((64, 8, 128), BF16), [SMEM, VMEM], [pltpu.VMEM((8, 1024), F32)])(
        val_index, val_orbitals.T
    )
    own = lax.all_to_all(piece, ("za", "zb", "yl", "yh"), 0, 0, tiled=True)
    orbital = cond_orbitals.astype(F32).reshape(4000, 128)
    low, high = index_parts(g_index)
    own, orbital = lax.optimization_barrier((own, orbital))
    chosen, done = call(chosen_kernel, (shape((256, NG), BF16), shape((8, 128), F32)), [VMEM], moved=2**23)(
        low.reshape(1, NG)
    )
    spread = call(spread_kernel, shape((4, 512, 128), BF16), [VMEM] * 2)(own.reshape(512, 128), done)
    own = lax.all_to_all(spread, "x", 0, 0, tiled=True).reshape(2048, 128)
    other = lax.ppermute(own, "core", [(0, 1), (1, 0)])
    first, second, third = tables()
    first, second, third = jnp.asarray(first, BF16), jnp.asarray(second, BF16), jnp.asarray(third, F32)
    grids = [pltpu.VMEM((2048, 128), F32), pltpu.VMEM((400, 640), BF16)]
    half = call(own_kernel, shape((320, 256), F32), [VMEM] * 4, grids)(own, orbital, first, second)
    values = call(
        values_kernel,
        shape((16, 40, 128), BF16),
        [SMEM] * 4 + [VMEM] * 8,
        grids + [pltpu.VMEM((80, 128), F32)] * 2,
    )(
        val_index, band_list, val_energy, cond_energy, half, other, orbital, chosen, high.reshape(1, NG),
        first, second, third,
    )
    gathered = lax.all_to_all(values, ("za", "yh"), 0, 0, tiled=True)
    packed = call(
        pack_kernel,
        shape((16, 16, 2816), BF16),
        [VMEM],
        [pltpu.VMEM((640, 128), F32), pltpu.VMEM((16, 5120), F32)],
    )(gathered)
    panel = lax.all_to_all(packed, ("zb", "yl", "x"), 0, 0, tiled=True).reshape(256, 2816)
    block = shape((80, 2560), F32)
    given = call(given_kernel, block, [VMEM])(panel)
    taken = lax.ppermute(given, "core", [(0, 1), (1, 0)])
    kept = call(kept_kernel, block, [VMEM] * 2)(panel, chi_old)
    return call(
        finish_kernel,
        block,
        [VMEM] * 2,
        [pltpu.VMEM((80, 2560), F32), pltpu.SemaphoreType.DMA((5,))],
        where=pl.BlockSpec(memory_space=pl.ANY),
    )(kept, taken)


def solution(mesh):
    fine = Mesh(mesh.devices.reshape(SIZES), AXES)
    every = AXES
    return jax.shard_map(
        body,
        mesh=fine,
        in_specs=(
            P(every, None),
            P(None, every),
            P(),
            P(),
            P(),
            P(every),
            P(),
            P(BAND + ("x",), "yh"),
        ),
        out_specs=P(BAND + ("x",), "yh"),
        check_vma=False,
    )
```

```python
import math

import jax
import jax.numpy as jnp
import numpy as np
from jax import lax
from jax.experimental import pallas as pl
from jax.experimental.pallas import tpu as pltpu
from jax.sharding import Mesh, PartitionSpec as P

NS = 80
NG = 10240
NCOND = 512
GRID = NS**3
PIECE = 1000
KEPT = 14
BF16 = jnp.bfloat16
F32 = jnp.float32
AXES = ("za", "zb", "yl", "core", "x", "yh")
SIZES = (4, 2, 2, 2, 4, 4)
BAND = ("za", "zb", "yl", "core")
VMEM = pl.BlockSpec(memory_space=pltpu.VMEM)
SMEM = pl.BlockSpec(memory_space=pltpu.SMEM)


def tables():
    freq = np.arange(KEPT)
    angle = 2 * np.pi * np.outer(np.arange(NS), freq) / NS
    along_z = np.zeros((NS, 32))
    along_z[:, :KEPT] = np.cos(angle)
    along_z[:, 16 : 16 + KEPT] = np.sin(angle)
    first = np.kron(np.eye(8), along_z)
    core, row = np.divmod(np.arange(800), 400)
    line = 25 * (2 * (row % 16) + core) + row // 16
    angle = 2 * np.pi * np.outer(freq, line // 10) / NS
    along_x = np.zeros((32, 800))
    along_x[:KEPT] = np.cos(angle)
    along_x[16 : 16 + KEPT] = np.sin(angle)
    tens = line % 10
    along_q = np.concatenate(
        [
            np.cos(2 * np.pi * np.outer(np.arange(6), tens) / 10),
            np.sin(2 * np.pi * np.outer(np.arange(1, 5), tens) / 10),
        ]
    )
    second = (along_q[:, None, :] * along_x[None]).reshape(320, 2, 400).transpose(1, 0, 2)
    angle = 2 * np.pi * np.outer(freq, np.arange(256) // 32) / NS
    third = np.zeros((32, 256))
    third[:KEPT] = np.cos(angle)
    third[16 : 16 + KEPT] = np.sin(angle)
    return first, second, third


def segments(m):
    found, lane = [], 0
    while lane < 128:
        piece, inside = divmod(128 * m + lane, PIECE)
        row, start = divmod(inside, 128)
        found.append((piece, row, lane))
        lane += min(128 - lane, 128 - start, PIECE - inside)
    return found


def index_parts(g_index):
    freq_z = g_index % NS
    freq_y = g_index // NS % NS
    freq_x = g_index // (NS * NS)

    def signed(freq):
        return jnp.where(freq > NS // 2, freq - NS, freq)

    x, y, z = signed(freq_x), signed(freq_y), signed(freq_z)
    sign = (x < 0).astype(jnp.int32) + 2 * (y < 0) + 4 * (z < 0)
    high = (jnp.abs(y) // 2) * 16 + jnp.abs(x)
    low = (jnp.abs(y) % 2) * 128 + sign * 16 + jnp.abs(z)
    return low, high


def widen_kernel(cond_ref, out_ref, done_ref):
    out_ref[...] = cond_ref[...].astype(F32).reshape(out_ref.shape)
    done_ref[...] = jnp.zeros((8, 128), F32)


def half_grid(core, valence_ref, cond_ref, first_ref, second_ref, val, block):
    val[...] = valence_ref[...].astype(F32)
    lane = lax.broadcasted_iota(jnp.int32, (16, 128), 1)
    turned = {}

    def turn(piece, row):
        if (piece, row) not in turned:
            at = piece // 4 * 512 + piece % 4 * 8 + row
            found = val[pl.ds(at, 16, stride=32), :]
            shift = 104 * piece % 128
            turned[piece, row] = pltpu.roll(found, shift, 1) if shift else found
        return turned[piece, row]

    parts = []
    for n in range(25):
        for t in range(5):
            m = 5 * n + t
            valence = None
            for piece, row, begin in segments(m):
                found = turn(piece, row)
                valence = found if valence is None else jnp.where(lane >= begin, found, valence)
            orbital = cond_ref[pl.ds(m + 125 * core, 16, stride=250), :]
            block[16 * n : 16 * n + 16, 128 * t : 128 * t + 128] = (valence * orbital).astype(BF16)
        if n % 5 == 4:
            parts.append(
                jnp.dot(
                    block[16 * (n - 4) : 16 * (n + 1), :],
                    first_ref[...],
                    preferred_element_type=F32,
                ).astype(BF16)
            )
    return jnp.dot(second_ref[core], jnp.concatenate(parts, axis=0), preferred_element_type=F32)


def own_kernel(own_ref, cond_ref, first_ref, second_ref, out_ref, val, block):
    core = lax.axis_index("core")
    out_ref[...] = half_grid(core, own_ref, cond_ref, first_ref, second_ref, val, block)


def values_kernel(
    pick_ref, number_ref, val_energy_ref, cond_energy_ref, half_ref, other_ref, cond_ref, chosen_ref, high_ref,
    first_ref, second_ref, third_ref, out_ref, val, block, rows, scaled,
):
    e_val = jnp.full((1, 128), val_energy_ref[pick_ref[0]], F32)
    e_cond = jnp.full((1, 128), cond_energy_ref[number_ref[0]], F32)
    weight = 4.0 / ((e_val - e_cond) * math.sqrt(NCOND))
    core = 1 - lax.axis_index("core")
    second = half_ref[...] + half_grid(core, other_ref, cond_ref, first_ref, second_ref, val, block)

    lane = lax.broadcasted_iota(jnp.int32, (16, 128), 1)
    group = lane // 16
    even = group % 2 == 0
    sx = jnp.where(group & 1 == 0, 1.0, -1.0)
    sy = jnp.where(group & 2 == 0, 1.0, -1.0)
    sz = jnp.where(group & 4 == 0, 1.0, -1.0)
    sxy, sxz, syz = sx * sy, sx * sz, sy * sz
    sxyz = sxy * sz

    def add_lanes(value):
        value = value[:, :128] + value[:, 128:]
        value = value + pltpu.roll(value, 64, 1)
        return value + pltpu.roll(value, 32, 1)

    def split(value):
        other = pltpu.roll(value, 16, 1)
        found = []
        for begin in (0, 16):
            a, b = value[begin : begin + 16], other[begin : begin + 16]
            found += [jnp.where(even, a, b), jnp.where(even, b, a)]
        return found

    planes = []
    for gy in range(KEPT):
        digit, sign = gy % 10, 1.0
        if digit > 5:
            digit, sign = 10 - digit, -1.0
        cosine, sine = third_ref[gy : gy + 1, :], third_ref[16 + gy : 17 + gy, :]
        even_q = second[32 * digit : 32 * digit + 32]
        re, im = even_q * cosine, even_q * sine
        if 1 <= digit <= 4:
            odd_q = second[32 * (digit + 5) : 32 * (digit + 5) + 32]
            re, im = re - (sign * sine) * odd_q, im + (sign * cosine) * odd_q
        ccc, ccs, scc, scs = split(add_lanes(re))
        csc, css, ssc, sss = split(add_lanes(im))
        total = (
            (ccc - syz * css) + (sz * ccs + sy * csc) + (sx * scc - sxz * scs) - (sxy * ssc + sxyz * sss)
        )
        planes.append((total * (1.0 / math.sqrt(GRID))).astype(BF16))
    cube = jnp.concatenate(
        [jnp.concatenate(planes[2 * i : 2 * i + 2], axis=1) for i in range(7)], axis=0
    )

    width = 1280
    place = lax.broadcasted_iota(jnp.int32, (112, width), 0)
    for c in range(NG // width):
        part = slice(c * width, (c + 1) * width)
        found = jnp.dot(cube, chosen_ref[:, part], preferred_element_type=F32)
        found = jnp.sum(jnp.where(place == high_ref[:, part], found, 0.0), axis=0, keepdims=True)
        found = found.astype(BF16).astype(F32)
        for k in range(width // 128):
            at = c * (width // 128) + k
            piece = found[:, 128 * k : 128 * k + 128]
            rows[at : at + 1, :] = piece
            scaled[at : at + 1, :] = weight * piece
    for k in range(16):
        yh, za = k % 4, k // 4
        out_ref[k] = jnp.concatenate(
            [rows[20 * yh : 20 * yh + 20, :], scaled[20 * za : 20 * za + 20, :]], axis=0
        ).astype(BF16)


def chosen_kernel(low_ref, out_ref):
    width = 1280
    inner = lax.broadcasted_iota(jnp.int32, (256, width), 0)
    for c in range(NG // width):
        part = slice(c * width, (c + 1) * width)
        out_ref[:, part] = jnp.where(inner == low_ref[:, part], 1.0, 0.0).astype(BF16)


def spread_kernel(own_ref, done_ref, out_ref):
    for k in range(4):
        out_ref[k] = own_ref[...]


def pack_kernel(h_ref, out_ref, wide, full):
    wide[...] = h_ref[...].reshape(16 * 40, 128).astype(F32)
    for k in range(40):
        full[:, 128 * k : 128 * k + 128] = wide[pl.ds(k, 16, stride=40), :]
    cols = full[:, 0:2560].astype(BF16)
    lane = lax.broadcasted_iota(jnp.int32, (16, 128), 1)
    core = lax.axis_index("core")
    for k in range(16):
        out_ref[k, :, 0:2560] = cols
        pieces = []
        for c in range(2):
            begin = 80 * (k // 4 * 8 + 4 * c + k % 4)
            first, shift = 2560 + begin // 128 * 128, begin % 128
            found = full[:, first : first + 128]
            if shift:
                found = pltpu.roll(found, 128 - shift, 1)
                if shift > 48:
                    after = pltpu.roll(full[:, first + 128 : first + 256], 128 - shift, 1)
                    found = jnp.where(lane < 128 - shift, found, after)
            pieces.append(found)
        mine = jnp.where(core == 0, pieces[0], pieces[1])
        theirs = jnp.where(core == 0, pieces[1], pieces[0])
        out_ref[k, :, 2560:2688] = mine.astype(BF16)
        out_ref[k, :, 2688:2816] = theirs.astype(BF16)


def times(left, right):
    return lax.dot_general(left, right, (((0,), (0,)), ((), ())), preferred_element_type=F32)[0:80]


def given_kernel(all_ref, out_ref):
    out_ref[...] = times(all_ref[:, 2688:2816], all_ref[:, 0:2560])


def kept_kernel(all_ref, chi_ref, out_ref):
    out_ref[...] = chi_ref[...] + times(all_ref[:, 2560:2688], all_ref[:, 0:2560])


def finish_kernel(kept_ref, taken_ref, out_ref, total, sent):
    copies = []
    for k in range(5):
        part = pl.ds(16 * k, 16)
        total[part, :] = kept_ref[part, :] + taken_ref[part, :]
        copies.append(pltpu.make_async_copy(total.at[part], out_ref.at[part], sent.at[k]))
        copies[-1].start()
    for copy in copies:
        copy.wait()


def call(kernel, out, in_specs, scratch=(), mib=16, flops=0, moved=0, where=VMEM):
    return pl.pallas_call(
        kernel,
        out_shape=out,
        in_specs=in_specs,
        out_specs=jax.tree.map(lambda _: where, out),
        scratch_shapes=scratch,
        compiler_params=pltpu.CompilerParams(vmem_limit_bytes=mib * 2**20),
        cost_estimate=pl.CostEstimate(flops=flops, bytes_accessed=moved, transcendentals=0),
    )


def body(cond_orbitals, val_orbitals, val_index, val_energy, cond_energy, band_list, g_index, chi_old):
    shape = jax.ShapeDtypeStruct
    piece = lax.dynamic_index_in_dim(val_orbitals, val_index[0], 0, keepdims=False)
    piece = jnp.pad(piece, (0, 24)).reshape(1, 8, 128)
    own = lax.all_to_all(
        jnp.broadcast_to(piece, (64, 8, 128)), ("za", "zb", "yl", "yh"), 0, 0, tiled=True
    )
    orbital, done = call(widen_kernel, (shape((4000, 128), F32), shape((8, 128), F32)), [VMEM])(cond_orbitals)
    low, high = index_parts(g_index)
    own, low, high = lax.optimization_barrier((own, low, high))
    chosen = call(chosen_kernel, shape((256, NG), BF16), [VMEM])(low.reshape(1, NG))
    spread = call(spread_kernel, shape((4, 512, 128), BF16), [VMEM] * 2)(own.reshape(512, 128), done)
    own = lax.all_to_all(spread, "x", 0, 0, tiled=True).reshape(2048, 128)
    other = lax.ppermute(own, "core", [(0, 1), (1, 0)])
    first, second, third = tables()
    first, second, third = jnp.asarray(first, BF16), jnp.asarray(second, BF16), jnp.asarray(third, F32)
    grids = [pltpu.VMEM((2048, 128), F32), pltpu.VMEM((400, 640), BF16)]
    half = call(own_kernel, shape((320, 256), F32), [VMEM] * 4, grids)(own, orbital, first, second)
    values = call(
        values_kernel,
        shape((16, 40, 128), BF16),
        [SMEM] * 4 + [VMEM] * 8,
        grids + [pltpu.VMEM((80, 128), F32)] * 2,
    )(
        val_index, band_list, val_energy, cond_energy, half, other, orbital, chosen, high.reshape(1, NG),
        first, second, third,
    )
    gathered = lax.all_to_all(values, ("za", "yh"), 0, 0, tiled=True)
    packed = call(
        pack_kernel,
        shape((16, 16, 2816), BF16),
        [VMEM],
        [pltpu.VMEM((640, 128), F32), pltpu.VMEM((16, 5120), F32)],
    )(gathered)
    panel = lax.all_to_all(packed, ("zb", "yl", "x"), 0, 0, tiled=True).reshape(256, 2816)
    block = shape((80, 2560), F32)
    given = call(given_kernel, block, [VMEM])(panel)
    taken = lax.ppermute(given, "core", [(0, 1), (1, 0)])
    kept = call(kept_kernel, block, [VMEM] * 2)(panel, chi_old)
    return call(
        finish_kernel,
        block,
        [VMEM] * 2,
        [pltpu.VMEM((80, 2560), F32), pltpu.SemaphoreType.DMA((5,))],
        where=pl.BlockSpec(memory_space=pl.ANY),
    )(kept, taken)


def solution(mesh):
    fine = Mesh(mesh.devices.reshape(SIZES), AXES)
    every = AXES
    return jax.shard_map(
        body,
        mesh=fine,
        in_specs=(
            P(every, None),
            P(None, every),
            P(),
            P(),
            P(),
            P(every),
            P(),
            P(BAND + ("x",), "yh"),
        ),
        out_specs=P(BAND + ("x",), "yh"),
        check_vma=False,
    )
```

```python
import math

import jax
import jax.numpy as jnp
import numpy as np
from jax import lax
from jax.experimental import pallas as pl
from jax.experimental.pallas import tpu as pltpu
from jax.sharding import Mesh, PartitionSpec as P

NS = 80
NG = 10240
NCOND = 512
GRID = NS**3
PIECE = 1000
KEPT = 14
BF16 = jnp.bfloat16
F32 = jnp.float32
AXES = ("za", "zb", "yl", "core", "x", "yh")
SIZES = (4, 2, 2, 2, 4, 4)
BAND = ("za", "zb", "yl", "core")
VMEM = pl.BlockSpec(memory_space=pltpu.VMEM)
SMEM = pl.BlockSpec(memory_space=pltpu.SMEM)


def tables():
    freq = np.arange(KEPT)
    angle = 2 * np.pi * np.outer(np.arange(NS), freq) / NS
    along_z = np.zeros((NS, 32))
    along_z[:, :KEPT] = np.cos(angle)
    along_z[:, 16 : 16 + KEPT] = np.sin(angle)
    first = np.kron(np.eye(8), along_z)
    core, row = np.divmod(np.arange(800), 400)
    line = 25 * (2 * (row % 16) + core) + row // 16
    angle = 2 * np.pi * np.outer(freq, line // 10) / NS
    along_x = np.zeros((32, 800))
    along_x[:KEPT] = np.cos(angle)
    along_x[16 : 16 + KEPT] = np.sin(angle)
    tens = line % 10
    along_q = np.concatenate(
        [
            np.cos(2 * np.pi * np.outer(np.arange(6), tens) / 10),
            np.sin(2 * np.pi * np.outer(np.arange(1, 5), tens) / 10),
        ]
    )
    second = (along_q[:, None, :] * along_x[None]).reshape(320, 2, 400).transpose(1, 0, 2)
    angle = 2 * np.pi * np.outer(freq, np.arange(256) // 32) / NS
    third = np.zeros((32, 256))
    third[:KEPT] = np.cos(angle)
    third[16 : 16 + KEPT] = np.sin(angle)
    return first, second, third


def segments(m):
    found, lane = [], 0
    while lane < 128:
        piece, inside = divmod(128 * m + lane, PIECE)
        row, start = divmod(inside, 128)
        found.append((piece, row, lane))
        lane += min(128 - lane, 128 - start, PIECE - inside)
    return found


def index_parts(g_index):
    freq_z = g_index % NS
    freq_y = g_index // NS % NS
    freq_x = g_index // (NS * NS)

    def signed(freq):
        return jnp.where(freq > NS // 2, freq - NS, freq)

    x, y, z = signed(freq_x), signed(freq_y), signed(freq_z)
    sign = (x < 0).astype(jnp.int32) + 2 * (y < 0) + 4 * (z < 0)
    high = (jnp.abs(y) // 2) * 16 + jnp.abs(x)
    low = (jnp.abs(y) % 2) * 128 + sign * 16 + jnp.abs(z)
    return low, high


def widen_kernel(cond_ref, out_ref, done_ref):
    out_ref[...] = cond_ref[...].astype(F32).reshape(out_ref.shape)
    done_ref[...] = jnp.zeros((8, 128), F32)


def half_grid(core, valence_ref, cond_ref, first_ref, second_ref, val, block):
    val[...] = valence_ref[...].astype(F32)
    lane = lax.broadcasted_iota(jnp.int32, (16, 128), 1)
    turned = {}

    def turn(piece, row):
        if (piece, row) not in turned:
            at = piece // 4 * 512 + piece % 4 * 8 + row
            found = val[pl.ds(at, 16, stride=32), :]
            shift = 104 * piece % 128
            turned[piece, row] = pltpu.roll(found, shift, 1) if shift else found
        return turned[piece, row]

    parts = []
    for n in range(25):
        for t in range(5):
            m = 5 * n + t
            valence = None
            for piece, row, begin in segments(m):
                found = turn(piece, row)
                valence = found if valence is None else jnp.where(lane >= begin, found, valence)
            orbital = cond_ref[pl.ds(m + 125 * core, 16, stride=250), :]
            block[16 * n : 16 * n + 16, 128 * t : 128 * t + 128] = (valence * orbital).astype(BF16)
        if n % 5 == 4:
            parts.append(
                jnp.dot(
                    block[16 * (n - 4) : 16 * (n + 1), :],
                    first_ref[...],
                    preferred_element_type=F32,
                ).astype(BF16)
            )
    return jnp.dot(second_ref[core], jnp.concatenate(parts, axis=0), preferred_element_type=F32)


def own_kernel(own_ref, cond_ref, first_ref, second_ref, out_ref, val, block):
    core = lax.axis_index("core")
    out_ref[...] = half_grid(core, own_ref, cond_ref, first_ref, second_ref, val, block)


def values_kernel(
    pick_ref, number_ref, val_energy_ref, cond_energy_ref, half_ref, other_ref, cond_ref, chosen_ref, high_ref,
    first_ref, second_ref, third_ref, out_ref, val, block, rows, scaled,
):
    e_val = jnp.full((1, 128), val_energy_ref[pick_ref[0]], F32)
    e_cond = jnp.full((1, 128), cond_energy_ref[number_ref[0]], F32)
    weight = 4.0 / ((e_val - e_cond) * math.sqrt(NCOND))
    core = 1 - lax.axis_index("core")
    second = half_ref[...] + half_grid(core, other_ref, cond_ref, first_ref, second_ref, val, block)

    lane = lax.broadcasted_iota(jnp.int32, (16, 128), 1)
    group = lane // 16
    even = group % 2 == 0
    sx = jnp.where(group & 1 == 0, 1.0, -1.0)
    sy = jnp.where(group & 2 == 0, 1.0, -1.0)
    sz = jnp.where(group & 4 == 0, 1.0, -1.0)
    sxy, sxz, syz = sx * sy, sx * sz, sy * sz
    sxyz = sxy * sz

    def add_lanes(value):
        value = value[:, :128] + value[:, 128:]
        value = value + pltpu.roll(value, 64, 1)
        return value + pltpu.roll(value, 32, 1)

    def split(value):
        other = pltpu.roll(value, 16, 1)
        found = []
        for begin in (0, 16):
            a, b = value[begin : begin + 16], other[begin : begin + 16]
            found += [jnp.where(even, a, b), jnp.where(even, b, a)]
        return found

    planes = []
    for gy in range(KEPT):
        digit, sign = gy % 10, 1.0
        if digit > 5:
            digit, sign = 10 - digit, -1.0
        cosine, sine = third_ref[gy : gy + 1, :], third_ref[16 + gy : 17 + gy, :]
        even_q = second[32 * digit : 32 * digit + 32]
        re, im = even_q * cosine, even_q * sine
        if 1 <= digit <= 4:
            odd_q = second[32 * (digit + 5) : 32 * (digit + 5) + 32]
            re, im = re - (sign * sine) * odd_q, im + (sign * cosine) * odd_q
        ccc, ccs, scc, scs = split(add_lanes(re))
        csc, css, ssc, sss = split(add_lanes(im))
        total = (
            (ccc - syz * css) + (sz * ccs + sy * csc) + (sx * scc - sxz * scs) - (sxy * ssc + sxyz * sss)
        )
        planes.append((total * (1.0 / math.sqrt(GRID))).astype(BF16))
    cube = jnp.concatenate(
        [jnp.concatenate(planes[2 * i : 2 * i + 2], axis=1) for i in range(7)], axis=0
    )

    width = 1280
    place = lax.broadcasted_iota(jnp.int32, (112, width), 0)
    for c in range(NG // width):
        part = slice(c * width, (c + 1) * width)
        found = jnp.dot(cube, chosen_ref[:, part], preferred_element_type=F32)
        found = jnp.sum(jnp.where(place == high_ref[:, part], found, 0.0), axis=0, keepdims=True)
        found = found.astype(BF16).astype(F32)
        for k in range(width // 128):
            at = c * (width // 128) + k
            piece = found[:, 128 * k : 128 * k + 128]
            rows[at : at + 1, :] = piece
            scaled[at : at + 1, :] = weight * piece
    for k in range(16):
        yh, za = k % 4, k // 4
        out_ref[k] = jnp.concatenate(
            [rows[20 * yh : 20 * yh + 20, :], scaled[20 * za : 20 * za + 20, :]], axis=0
        ).astype(BF16)


def chosen_kernel(low_ref, out_ref, done_ref):
    width = 1280
    done_ref[...] = jnp.zeros((8, 128), F32)
    inner = lax.broadcasted_iota(jnp.int32, (256, width), 0)
    for c in range(NG // width):
        part = slice(c * width, (c + 1) * width)
        out_ref[:, part] = jnp.where(inner == low_ref[:, part], 1.0, 0.0).astype(BF16)


def spread_kernel(own_ref, done_ref, also_ref, out_ref):
    for k in range(4):
        out_ref[k] = own_ref[...]


def pack_kernel(h_ref, out_ref, wide, full):
    wide[...] = h_ref[...].reshape(16 * 40, 128).astype(F32)
    for k in range(40):
        full[:, 128 * k : 128 * k + 128] = wide[pl.ds(k, 16, stride=40), :]
    cols = full[:, 0:2560].astype(BF16)
    lane = lax.broadcasted_iota(jnp.int32, (16, 128), 1)
    core = lax.axis_index("core")
    for k in range(16):
        out_ref[k, :, 0:2560] = cols
        pieces = []
        for c in range(2):
            begin = 80 * (k // 4 * 8 + 4 * c + k % 4)
            first, shift = 2560 + begin // 128 * 128, begin % 128
            found = full[:, first : first + 128]
            if shift:
                found = pltpu.roll(found, 128 - shift, 1)
                if shift > 48:
                    after = pltpu.roll(full[:, first + 128 : first + 256], 128 - shift, 1)
                    found = jnp.where(lane < 128 - shift, found, after)
            pieces.append(found)
        mine = jnp.where(core == 0, pieces[0], pieces[1])
        theirs = jnp.where(core == 0, pieces[1], pieces[0])
        out_ref[k, :, 2560:2688] = mine.astype(BF16)
        out_ref[k, :, 2688:2816] = theirs.astype(BF16)


def times(left, right):
    return lax.dot_general(left, right, (((0,), (0,)), ((), ())), preferred_element_type=F32)[0:80]


def given_kernel(all_ref, out_ref):
    out_ref[...] = times(all_ref[:, 2688:2816], all_ref[:, 0:2560]).astype(BF16)


def kept_kernel(all_ref, chi_ref, out_ref):
    out_ref[...] = chi_ref[...] + times(all_ref[:, 2560:2688], all_ref[:, 0:2560])


def finish_kernel(kept_ref, taken_ref, out_ref, total, sent):
    copies = []
    for k in range(5):
        part = pl.ds(16 * k, 16)
        total[part, :] = kept_ref[part, :] + taken_ref[part, :].astype(F32)
        copies.append(pltpu.make_async_copy(total.at[part], out_ref.at[part], sent.at[k]))
        copies[-1].start()
    for copy in copies:
        copy.wait()


def call(kernel, out, in_specs, scratch=(), mib=16, flops=0, moved=0, where=VMEM):
    return pl.pallas_call(
        kernel,
        out_shape=out,
        in_specs=in_specs,
        out_specs=jax.tree.map(lambda _: where, out),
        scratch_shapes=scratch,
        compiler_params=pltpu.CompilerParams(vmem_limit_bytes=mib * 2**20),
        cost_estimate=pl.CostEstimate(flops=flops, bytes_accessed=moved, transcendentals=0),
    )


def body(cond_orbitals, val_orbitals, val_index, val_energy, cond_energy, band_list, g_index, chi_old):
    shape = jax.ShapeDtypeStruct
    piece = lax.dynamic_index_in_dim(val_orbitals, val_index[0], 0, keepdims=False)
    piece = jnp.pad(piece, (0, 24)).reshape(1, 8, 128)
    own = lax.all_to_all(
        jnp.broadcast_to(piece, (64, 8, 128)), ("za", "zb", "yl", "yh"), 0, 0, tiled=True
    )
    orbital, done = call(widen_kernel, (shape((4000, 128), F32), shape((8, 128), F32)), [VMEM])(cond_orbitals)
    low, high = index_parts(g_index)
    chosen, also = call(chosen_kernel, (shape((256, NG), BF16), shape((8, 128), F32)), [VMEM])(low.reshape(1, NG))
    own, high = lax.optimization_barrier((own, high))
    spread = call(spread_kernel, shape((4, 512, 128), BF16), [VMEM] * 3)(own.reshape(512, 128), done, also)
    own = lax.all_to_all(spread, "x", 0, 0, tiled=True).reshape(2048, 128)
    other = lax.ppermute(own, "core", [(0, 1), (1, 0)])
    first, second, third = tables()
    first, second, third = jnp.asarray(first, BF16), jnp.asarray(second, BF16), jnp.asarray(third, F32)
    grids = [pltpu.VMEM((2048, 128), F32), pltpu.VMEM((400, 640), BF16)]
    half = call(own_kernel, shape((320, 256), F32), [VMEM] * 4, grids)(own, orbital, first, second)
    values = call(
        values_kernel,
        shape((16, 40, 128), BF16),
        [SMEM] * 4 + [VMEM] * 8,
        grids + [pltpu.VMEM((80, 128), F32)] * 2,
    )(
        val_index, band_list, val_energy, cond_energy, half, other, orbital, chosen, high.reshape(1, NG),
        first, second, third,
    )
    gathered = lax.all_to_all(values, ("za", "yh"), 0, 0, tiled=True)
    packed = call(
        pack_kernel,
        shape((16, 16, 2816), BF16),
        [VMEM],
        [pltpu.VMEM((640, 128), F32), pltpu.VMEM((16, 5120), F32)],
    )(gathered)
    panel = lax.all_to_all(packed, ("zb", "yl", "x"), 0, 0, tiled=True).reshape(256, 2816)
    block = shape((80, 2560), F32)
    given = call(given_kernel, shape((80, 2560), BF16), [VMEM])(panel)
    taken = lax.ppermute(given, "core", [(0, 1), (1, 0)])
    kept = call(kept_kernel, block, [VMEM] * 2)(panel, chi_old)
    return call(
        finish_kernel,
        block,
        [VMEM] * 2,
        [pltpu.VMEM((80, 2560), F32), pltpu.SemaphoreType.DMA((5,))],
        where=pl.BlockSpec(memory_space=pl.ANY),
    )(kept, taken)


def solution(mesh):
    fine = Mesh(mesh.devices.reshape(SIZES), AXES)
    every = AXES
    return jax.shard_map(
        body,
        mesh=fine,
        in_specs=(
            P(every, None),
            P(None, every),
            P(),
            P(),
            P(),
            P(every),
            P(),
            P(BAND + ("x",), "yh"),
        ),
        out_specs=P(BAND + ("x",), "yh"),
        check_vma=False,
    )
```

```python
import math

import jax
import jax.numpy as jnp
import numpy as np
from jax import lax
from jax.experimental import pallas as pl
from jax.experimental.pallas import tpu as pltpu
from jax.sharding import Mesh, PartitionSpec as P

NS = 80
NG = 10240
NCOND = 512
GRID = NS**3
PIECE = 1000
KEPT = 14
BF16 = jnp.bfloat16
F32 = jnp.float32
AXES = ("za", "zb", "yl", "core", "x", "yh")
SIZES = (4, 2, 2, 2, 4, 4)
BAND = ("za", "zb", "yl", "core")
VMEM = pl.BlockSpec(memory_space=pltpu.VMEM)


def tables():
    freq = np.arange(KEPT)
    angle = 2 * np.pi * np.outer(np.arange(NS), freq) / NS
    along_z = np.zeros((NS, 32))
    along_z[:, :KEPT] = np.cos(angle)
    along_z[:, 16 : 16 + KEPT] = np.sin(angle)
    first = np.kron(np.eye(8), along_z)
    core, row = np.divmod(np.arange(800), 400)
    line = 25 * (2 * (row % 16) + core) + row // 16
    angle = 2 * np.pi * np.outer(freq, line // 10) / NS
    along_x = np.zeros((32, 800))
    along_x[:KEPT] = np.cos(angle)
    along_x[16 : 16 + KEPT] = np.sin(angle)
    tens = line % 10
    along_q = np.concatenate(
        [
            np.cos(2 * np.pi * np.outer(np.arange(6), tens) / 10),
            np.sin(2 * np.pi * np.outer(np.arange(1, 5), tens) / 10),
        ]
    )
    second = (along_q[:, None, :] * along_x[None]).reshape(320, 2, 400).transpose(1, 0, 2)
    angle = 2 * np.pi * np.outer(freq, np.arange(256) // 32) / NS
    third = np.zeros((32, 256))
    third[:KEPT] = np.cos(angle)
    third[16 : 16 + KEPT] = np.sin(angle)
    return first, second, third


def segments(m):
    found, lane = [], 0
    while lane < 128:
        piece, inside = divmod(128 * m + lane, PIECE)
        row, start = divmod(inside, 128)
        found.append((piece, row, lane))
        lane += min(128 - lane, 128 - start, PIECE - inside)
    return found


def index_parts(g_index):
    freq_z = g_index % NS
    freq_y = g_index // NS % NS
    freq_x = g_index // (NS * NS)

    def signed(freq):
        return jnp.where(freq > NS // 2, freq - NS, freq)

    x, y, z = signed(freq_x), signed(freq_y), signed(freq_z)
    sign = (x < 0).astype(jnp.int32) + 2 * (y < 0) + 4 * (z < 0)
    high = (jnp.abs(y) // 2) * 16 + jnp.abs(x)
    low = (jnp.abs(y) % 2) * 128 + sign * 16 + jnp.abs(z)
    return low, high


def one_of(values_ref, number_ref):
    match = lax.broadcasted_iota(jnp.int32, values_ref.shape, 1) == number_ref[...]
    return jnp.sum(jnp.where(match, values_ref[...], 0.0), axis=1, keepdims=True)


def widen_kernel(cond_ref, out_ref, done_ref, wide):
    wide[...] = cond_ref[...].astype(F32).reshape(wide.shape)
    for core in range(2):
        for m in range(125):
            out_ref[core, m] = wide[pl.ds(m + 125 * core, 16, stride=250), :]
    done_ref[...] = jnp.zeros((8, 128), F32)


def half_grid(core, valence_ref, cond_ref, first_ref, second_ref, block):
    lane = lax.broadcasted_iota(jnp.int32, (16, 128), 1)
    turned = {}

    def turn(piece, row):
        if (piece, row) not in turned:
            at = 128 * piece + 16 * row
            found = valence_ref[at : at + 16, :].astype(F32)
            shift = 104 * piece % 128
            turned[piece, row] = pltpu.roll(found, shift, 1) if shift else found
        return turned[piece, row]

    parts = []
    for n in range(25):
        for t in range(5):
            m = 5 * n + t
            valence = None
            for piece, row, begin in segments(m):
                found = turn(piece, row)
                valence = found if valence is None else jnp.where(lane >= begin, found, valence)
            block[16 * n : 16 * n + 16, 128 * t : 128 * t + 128] = (valence * cond_ref[core, m]).astype(BF16)
        if n % 5 == 4:
            parts.append(
                jnp.dot(
                    block[16 * (n - 4) : 16 * (n + 1), :],
                    first_ref[...],
                    preferred_element_type=F32,
                ).astype(BF16)
            )
    return jnp.dot(second_ref[core], jnp.concatenate(parts, axis=0), preferred_element_type=F32)


def own_kernel(
    own_ref, cond_ref, first_ref, second_ref, pick_ref, number_ref, val_energy_ref, cond_energy_ref,
    out_ref, weight_ref, block,
):
    core = lax.axis_index("core")
    out_ref[...] = half_grid(core, own_ref, cond_ref, first_ref, second_ref, block)
    gap = one_of(val_energy_ref, pick_ref) - one_of(cond_energy_ref, number_ref)
    weight_ref[...] = jnp.broadcast_to(4.0 / (gap * math.sqrt(NCOND)), weight_ref.shape)


def values_kernel(
    weight_ref, half_ref, other_ref, cond_ref, chosen_ref, high_ref, first_ref, second_ref,
    third_ref, out_ref, block, rows, scaled,
):
    weight = weight_ref[0:1, :]
    core = 1 - lax.axis_index("core")
    second = half_ref[...] + half_grid(core, other_ref, cond_ref, first_ref, second_ref, block)

    lane = lax.broadcasted_iota(jnp.int32, (16, 128), 1)
    group = lane // 16
    even = group % 2 == 0
    sx = jnp.where(group & 1 == 0, 1.0, -1.0)
    sy = jnp.where(group & 2 == 0, 1.0, -1.0)
    sz = jnp.where(group & 4 == 0, 1.0, -1.0)
    sxy, sxz, syz = sx * sy, sx * sz, sy * sz
    sxyz = sxy * sz

    def add_lanes(value):
        value = value[:, :128] + value[:, 128:]
        value = value + pltpu.roll(value, 64, 1)
        return value + pltpu.roll(value, 32, 1)

    def split(value):
        other = pltpu.roll(value, 16, 1)
        found = []
        for begin in (0, 16):
            a, b = value[begin : begin + 16], other[begin : begin + 16]
            found += [jnp.where(even, a, b), jnp.where(even, b, a)]
        return found

    planes = []
    for gy in range(KEPT):
        digit, sign = gy % 10, 1.0
        if digit > 5:
            digit, sign = 10 - digit, -1.0
        cosine, sine = third_ref[gy : gy + 1, :], third_ref[16 + gy : 17 + gy, :]
        even_q = second[32 * digit : 32 * digit + 32]
        re, im = even_q * cosine, even_q * sine
        if 1 <= digit <= 4:
            odd_q = second[32 * (digit + 5) : 32 * (digit + 5) + 32]
            re, im = re - (sign * sine) * odd_q, im + (sign * cosine) * odd_q
        ccc, ccs, scc, scs = split(add_lanes(re))
        csc, css, ssc, sss = split(add_lanes(im))
        total = (
            (ccc - syz * css) + (sz * ccs + sy * csc) + (sx * scc - sxz * scs) - (sxy * ssc + sxyz * sss)
        )
        planes.append((total * (1.0 / math.sqrt(GRID))).astype(BF16))
    cube = jnp.concatenate(
        [jnp.concatenate(planes[2 * i : 2 * i + 2], axis=1) for i in range(7)], axis=0
    )

    width = 1280
    place = lax.broadcasted_iota(jnp.int32, (112, width), 0)
    for c in range(NG // width):
        part = slice(c * width, (c + 1) * width)
        found = jnp.dot(cube, chosen_ref[:, part], preferred_element_type=F32)
        found = jnp.sum(jnp.where(place == high_ref[:, part], found, 0.0), axis=0, keepdims=True)
        found = found.astype(BF16).astype(F32)
        for k in range(width // 128):
            at = c * (width // 128) + k
            piece = found[:, 128 * k : 128 * k + 128]
            rows[at : at + 1, :] = piece
            scaled[at : at + 1, :] = weight * piece
    for k in range(16):
        yh, za = k % 4, k // 4
        out_ref[k] = jnp.concatenate(
            [rows[20 * yh : 20 * yh + 20, :], scaled[20 * za : 20 * za + 20, :]], axis=0
        ).astype(BF16)


def chosen_kernel(low_ref, out_ref):
    width = 1280
    inner = lax.broadcasted_iota(jnp.int32, (256, width), 0)
    for c in range(NG // width):
        part = slice(c * width, (c + 1) * width)
        out_ref[:, part] = jnp.where(inner == low_ref[:, part], 1.0, 0.0).astype(BF16)


def spread_kernel(own_ref, done_ref, out_ref, wide):
    wide[...] = own_ref[...].astype(F32)
    for m in range(32):
        found = wide[pl.ds(m, 16, stride=32), :].astype(BF16)
        for k in range(4):
            out_ref[k, 16 * m : 16 * m + 16, :] = found


def pack_kernel(h_ref, out_ref, wide, full):
    wide[...] = h_ref[...].reshape(16 * 40, 128).astype(F32)
    for k in range(40):
        full[:, 128 * k : 128 * k + 128] = wide[pl.ds(k, 16, stride=40), :]
    cols = full[:, 0:2560].astype(BF16)
    lane = lax.broadcasted_iota(jnp.int32, (16, 128), 1)
    core = lax.axis_index("core")
    for k in range(16):
        out_ref[k, :, 0:2560] = cols
        pieces = []
        for c in range(2):
            begin = 80 * (k // 4 * 8 + 4 * c + k % 4)
            first, shift = 2560 + begin // 128 * 128, begin % 128
            found = full[:, first : first + 128]
            if shift:
                found = pltpu.roll(found, 128 - shift, 1)
                if shift > 48:
                    after = pltpu.roll(full[:, first + 128 : first + 256], 128 - shift, 1)
                    found = jnp.where(lane < 128 - shift, found, after)
            pieces.append(found)
        mine = jnp.where(core == 0, pieces[0], pieces[1])
        theirs = jnp.where(core == 0, pieces[1], pieces[0])
        out_ref[k, :, 2560:2688] = mine.astype(BF16)
        out_ref[k, :, 2688:2816] = theirs.astype(BF16)


def times(left, right):
    return lax.dot_general(left, right, (((0,), (0,)), ((), ())), preferred_element_type=F32)[0:80]


def given_kernel(all_ref, out_ref):
    out_ref[...] = times(all_ref[:, 2688:2816], all_ref[:, 0:2560]).astype(BF16)


def kept_kernel(all_ref, chi_ref, out_ref):
    out_ref[...] = chi_ref[...] + times(all_ref[:, 2560:2688], all_ref[:, 0:2560])


def finish_kernel(kept_ref, taken_ref, out_ref, total, sent):
    copies = []
    for k in range(5):
        part = pl.ds(16 * k, 16)
        total[part, :] = kept_ref[part, :] + taken_ref[part, :].astype(F32)
        copies.append(pltpu.make_async_copy(total.at[part], out_ref.at[part], sent.at[k]))
        copies[-1].start()
    for copy in copies:
        copy.wait()


def call(kernel, out, in_specs, scratch=(), mib=16, flops=0, moved=0, where=VMEM):
    return pl.pallas_call(
        kernel,
        out_shape=out,
        in_specs=in_specs,
        out_specs=jax.tree.map(lambda _: where, out),
        scratch_shapes=scratch,
        compiler_params=pltpu.CompilerParams(vmem_limit_bytes=mib * 2**20),
        cost_estimate=pl.CostEstimate(flops=flops, bytes_accessed=moved, transcendentals=0),
    )


def body(cond_orbitals, val_orbitals, val_index, val_energy, cond_energy, band_list, g_index, chi_old):
    shape = jax.ShapeDtypeStruct
    piece = lax.dynamic_index_in_dim(val_orbitals, val_index[0], 0, keepdims=False)
    piece = jnp.pad(piece, (0, 24)).reshape(1, 8, 128)
    own = lax.all_to_all(
        jnp.broadcast_to(piece, (64, 8, 128)), ("za", "zb", "yl", "yh"), 0, 0, tiled=True
    )
    orbital, done = call(
        widen_kernel,
        (shape((2, 125, 16, 128), F32), shape((8, 128), F32)),
        [VMEM],
        [pltpu.VMEM((4000, 128), F32)],
    )(cond_orbitals)
    low, high = index_parts(g_index)
    own, low, high = lax.optimization_barrier((own, low, high))
    chosen = call(chosen_kernel, shape((256, NG), BF16), [VMEM])(low.reshape(1, NG))
    spread = call(spread_kernel, shape((4, 512, 128), BF16), [VMEM] * 2, [pltpu.VMEM((512, 128), F32)])(own.reshape(512, 128), done)
    own = lax.all_to_all(spread, "x", 0, 0, tiled=True).reshape(2048, 128)
    other = lax.ppermute(own, "core", [(0, 1), (1, 0)])
    first, second, third = tables()
    first, second, third = jnp.asarray(first, BF16), jnp.asarray(second, BF16), jnp.asarray(third, F32)
    grids = [pltpu.VMEM((400, 640), BF16)]
    half, weight = call(own_kernel, (shape((320, 256), F32), shape((8, 128), F32)), [VMEM] * 8, grids)(
        own, orbital, first, second, val_index.reshape(1, 1), band_list.reshape(1, 1), val_energy.reshape(1, -1),
        cond_energy.reshape(1, -1),
    )
    values = call(
        values_kernel,
        shape((16, 40, 128), BF16),
        [VMEM] * 9,
        grids + [pltpu.VMEM((80, 128), F32)] * 2,
    )(
        weight, half, other, orbital, chosen, high.reshape(1, NG),
        first, second, third,
    )
    gathered = lax.all_to_all(values, ("za", "yh"), 0, 0, tiled=True)
    packed = call(
        pack_kernel,
        shape((16, 16, 2816), BF16),
        [VMEM],
        [pltpu.VMEM((640, 128), F32), pltpu.VMEM((16, 5120), F32)],
    )(gathered)
    panel = lax.all_to_all(packed, ("zb", "yl", "x"), 0, 0, tiled=True).reshape(256, 2816)
    block = shape((80, 2560), F32)
    given = call(given_kernel, shape((80, 2560), BF16), [VMEM])(panel)
    taken = lax.ppermute(given, "core", [(0, 1), (1, 0)])
    kept = call(kept_kernel, block, [VMEM] * 2)(panel, chi_old)
    return call(
        finish_kernel,
        block,
        [VMEM] * 2,
        [pltpu.VMEM((80, 2560), F32), pltpu.SemaphoreType.DMA((5,))],
        where=pl.BlockSpec(memory_space=pl.ANY),
    )(kept, taken)


def solution(mesh):
    fine = Mesh(mesh.devices.reshape(SIZES), AXES)
    every = AXES
    return jax.shard_map(
        body,
        mesh=fine,
        in_specs=(
            P(every, None),
            P(None, every),
            P(),
            P(),
            P(),
            P(every),
            P(),
            P(BAND + ("x",), "yh"),
        ),
        out_specs=P(BAND + ("x",), "yh"),
        check_vma=False,
    )
```

```python
import math

import jax
import jax.numpy as jnp
import numpy as np
from jax import lax
from jax.experimental import pallas as pl
from jax.experimental.pallas import tpu as pltpu
from jax.sharding import Mesh, PartitionSpec as P

NS = 80
NG = 10240
NCOND = 512
GRID = NS**3
PIECE = 1000
KEPT = 14
BF16 = jnp.bfloat16
F32 = jnp.float32
AXES = ("za", "zb", "yl", "core", "x", "yh")
SIZES = (4, 2, 2, 2, 4, 4)
BAND = ("za", "zb", "yl", "core")
VMEM = pl.BlockSpec(memory_space=pltpu.VMEM)


def tables():
    freq = np.arange(KEPT)
    angle = 2 * np.pi * np.outer(np.arange(NS), freq) / NS
    along_z = np.zeros((NS, 32))
    along_z[:, :KEPT] = np.cos(angle)
    along_z[:, 16 : 16 + KEPT] = np.sin(angle)
    first = np.kron(np.eye(8), along_z)
    core, row = np.divmod(np.arange(800), 400)
    line = 25 * (2 * (row % 16) + core) + row // 16
    angle = 2 * np.pi * np.outer(freq, line // 10) / NS
    along_x = np.zeros((32, 800))
    along_x[:KEPT] = np.cos(angle)
    along_x[16 : 16 + KEPT] = np.sin(angle)
    tens = line % 10
    along_q = np.concatenate(
        [
            np.cos(2 * np.pi * np.outer(np.arange(6), tens) / 10),
            np.sin(2 * np.pi * np.outer(np.arange(1, 5), tens) / 10),
        ]
    )
    second = (along_q[:, None, :] * along_x[None]).reshape(320, 2, 400).transpose(1, 0, 2)
    angle = 2 * np.pi * np.outer(freq, np.arange(256) // 32) / NS
    third = np.zeros((32, 256))
    third[:KEPT] = np.cos(angle)
    third[16 : 16 + KEPT] = np.sin(angle)
    return first, second, third


def segments(m):
    found, lane = [], 0
    while lane < 128:
        piece, inside = divmod(128 * m + lane, PIECE)
        row, start = divmod(inside, 128)
        found.append((piece, row, lane))
        lane += min(128 - lane, 128 - start, PIECE - inside)
    return found


def index_parts(g_index):
    freq_z = g_index % NS
    freq_y = g_index // NS % NS
    freq_x = g_index // (NS * NS)

    def signed(freq):
        return jnp.where(freq > NS // 2, freq - NS, freq)

    x, y, z = signed(freq_x), signed(freq_y), signed(freq_z)
    sign = (x < 0).astype(jnp.int32) + 2 * (y < 0) + 4 * (z < 0)
    high = (jnp.abs(y) // 2) * 16 + jnp.abs(x)
    low = (jnp.abs(y) % 2) * 128 + sign * 16 + jnp.abs(z)
    return low, high


def one_of(values_ref, number):
    match = lax.broadcasted_iota(jnp.int32, values_ref.shape, 1) == number
    return jnp.sum(jnp.where(match, values_ref[...], 0.0), axis=1, keepdims=True)


def widen_kernel(cond_ref, number_ref, out_ref, number_out_ref, wide):
    wide[...] = cond_ref[...].astype(F32).reshape(wide.shape)
    for core in range(2):
        for m in range(125):
            out_ref[core, m] = wide[pl.ds(m + 125 * core, 16, stride=250), :]
    number_out_ref[...] = jnp.broadcast_to(number_ref[...].reshape(1, 1), number_out_ref.shape)


def half_grid(core, valence_ref, cond_ref, first_ref, second_ref, block):
    lane = lax.broadcasted_iota(jnp.int32, (16, 128), 1)
    turned = {}

    def turn(piece, row):
        if (piece, row) not in turned:
            at = 128 * piece + 16 * row
            found = valence_ref[at : at + 16, :].astype(F32)
            shift = 104 * piece % 128
            turned[piece, row] = pltpu.roll(found, shift, 1) if shift else found
        return turned[piece, row]

    parts = []
    for n in range(25):
        for t in range(5):
            m = 5 * n + t
            valence = None
            for piece, row, begin in segments(m):
                found = turn(piece, row)
                valence = found if valence is None else jnp.where(lane >= begin, found, valence)
            block[16 * n : 16 * n + 16, 128 * t : 128 * t + 128] = (valence * cond_ref[core, m]).astype(BF16)
        if n % 5 == 4:
            parts.append(
                jnp.dot(
                    block[16 * (n - 4) : 16 * (n + 1), :],
                    first_ref[...],
                    preferred_element_type=F32,
                ).astype(BF16)
            )
    return jnp.dot(second_ref[core], jnp.concatenate(parts, axis=0), preferred_element_type=F32)


def own_kernel(
    own_ref, cond_ref, first_ref, second_ref, pick_ref, number_ref, val_energy_ref, cond_energy_ref,
    out_ref, weight_ref, block,
):
    core = lax.axis_index("core")
    out_ref[...] = half_grid(core, own_ref, cond_ref, first_ref, second_ref, block)
    e_val = one_of(val_energy_ref, pick_ref[...].reshape(1, 1))
    gap = e_val - one_of(cond_energy_ref, number_ref[0:1, 0:1])
    weight_ref[...] = jnp.broadcast_to(4.0 / (gap * math.sqrt(NCOND)), weight_ref.shape)


def values_kernel(
    weight_ref, half_ref, other_ref, cond_ref, chosen_ref, high_ref, first_ref, second_ref,
    third_ref, out_ref, block, rows, scaled,
):
    weight = weight_ref[0:1, :]
    core = 1 - lax.axis_index("core")
    second = half_ref[...] + half_grid(core, other_ref, cond_ref, first_ref, second_ref, block)

    lane = lax.broadcasted_iota(jnp.int32, (16, 128), 1)
    group = lane // 16
    even = group % 2 == 0
    sx = jnp.where(group & 1 == 0, 1.0, -1.0)
    sy = jnp.where(group & 2 == 0, 1.0, -1.0)
    sz = jnp.where(group & 4 == 0, 1.0, -1.0)
    sxy, sxz, syz = sx * sy, sx * sz, sy * sz
    sxyz = sxy * sz

    def add_lanes(value):
        value = value[:, :128] + value[:, 128:]
        value = value + pltpu.roll(value, 64, 1)
        return value + pltpu.roll(value, 32, 1)

    def split(value):
        other = pltpu.roll(value, 16, 1)
        found = []
        for begin in (0, 16):
            a, b = value[begin : begin + 16], other[begin : begin + 16]
            found += [jnp.where(even, a, b), jnp.where(even, b, a)]
        return found

    planes = []
    for gy in range(KEPT):
        digit, sign = gy % 10, 1.0
        if digit > 5:
            digit, sign = 10 - digit, -1.0
        cosine, sine = third_ref[gy : gy + 1, :], third_ref[16 + gy : 17 + gy, :]
        even_q = second[32 * digit : 32 * digit + 32]
        re, im = even_q * cosine, even_q * sine
        if 1 <= digit <= 4:
            odd_q = second[32 * (digit + 5) : 32 * (digit + 5) + 32]
            re, im = re - (sign * sine) * odd_q, im + (sign * cosine) * odd_q
        ccc, ccs, scc, scs = split(add_lanes(re))
        csc, css, ssc, sss = split(add_lanes(im))
        total = (
            (ccc - syz * css) + (sz * ccs + sy * csc) + (sx * scc - sxz * scs) - (sxy * ssc + sxyz * sss)
        )
        planes.append((total * (1.0 / math.sqrt(GRID))).astype(BF16))
    cube = jnp.concatenate(
        [jnp.concatenate(planes[2 * i : 2 * i + 2], axis=1) for i in range(7)], axis=0
    )

    width = 1280
    place = lax.broadcasted_iota(jnp.int32, (112, width), 0)
    for c in range(NG // width):
        part = slice(c * width, (c + 1) * width)
        found = jnp.dot(cube, chosen_ref[:, part], preferred_element_type=F32)
        found = jnp.sum(jnp.where(place == high_ref[:, part], found, 0.0), axis=0, keepdims=True)
        found = found.astype(BF16).astype(F32)
        for k in range(width // 128):
            at = c * (width // 128) + k
            piece = found[:, 128 * k : 128 * k + 128]
            rows[at : at + 1, :] = piece
            scaled[at : at + 1, :] = weight * piece
    for k in range(16):
        yh, za = k % 4, k // 4
        out_ref[k] = jnp.concatenate(
            [rows[20 * yh : 20 * yh + 20, :], scaled[20 * za : 20 * za + 20, :]], axis=0
        ).astype(BF16)


def chosen_kernel(low_ref, out_ref):
    width = 1280
    inner = lax.broadcasted_iota(jnp.int32, (256, width), 0)
    for c in range(NG // width):
        part = slice(c * width, (c + 1) * width)
        out_ref[:, part] = jnp.where(inner == low_ref[:, part], 1.0, 0.0).astype(BF16)


def spread_kernel(own_ref, number_ref, out_ref, wide):
    wide[...] = own_ref[...].astype(F32)
    for m in range(32):
        found = wide[pl.ds(m, 16, stride=32), :].astype(BF16)
        for k in range(4):
            out_ref[k, 16 * m : 16 * m + 16, :] = found


def pack_kernel(h_ref, out_ref, wide, full):
    wide[...] = h_ref[...].reshape(16 * 40, 128).astype(F32)
    for k in range(40):
        full[:, 128 * k : 128 * k + 128] = wide[pl.ds(k, 16, stride=40), :]
    cols = full[:, 0:2560].astype(BF16)
    lane = lax.broadcasted_iota(jnp.int32, (16, 128), 1)
    core = lax.axis_index("core")
    for k in range(16):
        out_ref[k, :, 0:2560] = cols
        pieces = []
        for c in range(2):
            begin = 80 * (k % 4 * 8 + 4 * c + k // 4)
            first, shift = 2560 + begin // 128 * 128, begin % 128
            found = full[:, first : first + 128]
            if shift:
                found = pltpu.roll(found, 128 - shift, 1)
                if shift > 48:
                    after = pltpu.roll(full[:, first + 128 : first + 256], 128 - shift, 1)
                    found = jnp.where(lane < 128 - shift, found, after)
            pieces.append(found)
        mine = jnp.where(core == 0, pieces[0], pieces[1])
        theirs = jnp.where(core == 0, pieces[1], pieces[0])
        out_ref[k, :, 2560:2688] = mine.astype(BF16)
        out_ref[k, :, 2688:2816] = theirs.astype(BF16)


def times(left, right):
    return lax.dot_general(left, right, (((0,), (0,)), ((), ())), preferred_element_type=F32)[0:80]


def given_kernel(all_ref, out_ref):
    out_ref[...] = times(all_ref[:, 2688:2816], all_ref[:, 0:2560]).astype(BF16)


def kept_kernel(all_ref, chi_ref, out_ref):
    out_ref[...] = chi_ref[...] + times(all_ref[:, 2560:2688], all_ref[:, 0:2560])


def finish_kernel(kept_ref, taken_ref, out_ref, total, sent):
    copies = []
    for k in range(5):
        part = pl.ds(16 * k, 16)
        total[part, :] = kept_ref[part, :] + taken_ref[part, :].astype(F32)
        copies.append(pltpu.make_async_copy(total.at[part], out_ref.at[part], sent.at[k]))
        copies[-1].start()
    for copy in copies:
        copy.wait()


def call(kernel, out, in_specs, scratch=(), mib=16, flops=0, moved=0, where=VMEM):
    return pl.pallas_call(
        kernel,
        out_shape=out,
        in_specs=in_specs,
        out_specs=jax.tree.map(lambda _: where, out),
        scratch_shapes=scratch,
        compiler_params=pltpu.CompilerParams(vmem_limit_bytes=mib * 2**20),
        cost_estimate=pl.CostEstimate(flops=flops, bytes_accessed=moved, transcendentals=0),
    )


def body(cond_orbitals, val_orbitals, val_index, val_energy, cond_energy, band_list, g_index, chi_old):
    shape = jax.ShapeDtypeStruct
    piece = lax.dynamic_index_in_dim(val_orbitals, val_index[0], 0, keepdims=False)
    piece = jnp.pad(piece, (0, 24)).reshape(1, 8, 128)
    own = lax.all_to_all(
        jnp.broadcast_to(piece, (64, 8, 128)), ("za", "zb", "yl", "yh"), 0, 0, tiled=True
    )
    orbital, number = call(
        widen_kernel,
        (shape((2, 125, 16, 128), F32), shape((8, 128), jnp.int32)),
        [VMEM] * 2,
        [pltpu.VMEM((4000, 128), F32)],
    )(cond_orbitals, band_list)
    low, high = index_parts(g_index)
    own, low, high = lax.optimization_barrier((own, low, high))
    chosen = call(chosen_kernel, shape((256, NG), BF16), [VMEM])(low.reshape(1, NG))
    spread = call(spread_kernel, shape((4, 512, 128), BF16), [VMEM] * 2, [pltpu.VMEM((512, 128), F32)])(own.reshape(512, 128), number)
    own = lax.all_to_all(spread, "x", 0, 0, tiled=True).reshape(2048, 128)
    other = lax.ppermute(own, "core", [(0, 1), (1, 0)])
    first, second, third = tables()
    first, second, third = jnp.asarray(first, BF16), jnp.asarray(second, BF16), jnp.asarray(third, F32)
    grids = [pltpu.VMEM((400, 640), BF16)]
    half, weight = call(own_kernel, (shape((320, 256), F32), shape((8, 128), F32)), [VMEM] * 8, grids)(
        own, orbital, first, second, val_index, number, val_energy.reshape(1, -1),
        cond_energy.reshape(1, -1),
    )
    values = call(
        values_kernel,
        shape((16, 40, 128), BF16),
        [VMEM] * 9,
        grids + [pltpu.VMEM((80, 128), F32)] * 2,
    )(
        weight, half, other, orbital, chosen, high.reshape(1, NG),
        first, second, third,
    )
    gathered = lax.all_to_all(values, ("za", "yh"), 0, 0, tiled=True)
    packed = call(
        pack_kernel,
        shape((16, 16, 2816), BF16),
        [VMEM],
        [pltpu.VMEM((640, 128), F32), pltpu.VMEM((16, 5120), F32)],
    )(gathered)
    panel = lax.all_to_all(packed, ("x", "zb", "yl"), 0, 0, tiled=True).reshape(256, 2816)
    block = shape((80, 2560), F32)
    given = call(given_kernel, shape((80, 2560), BF16), [VMEM])(panel)
    taken = lax.ppermute(given, "core", [(0, 1), (1, 0)])
    kept = call(kept_kernel, block, [VMEM] * 2)(panel, chi_old)
    return call(
        finish_kernel,
        block,
        [VMEM] * 2,
        [pltpu.VMEM((80, 2560), F32), pltpu.SemaphoreType.DMA((5,))],
        where=pl.BlockSpec(memory_space=pl.ANY),
    )(kept, taken)


def solution(mesh):
    fine = Mesh(mesh.devices.reshape(SIZES), AXES)
    every = AXES
    return jax.shard_map(
        body,
        mesh=fine,
        in_specs=(
            P(every, None),
            P(None, every),
            P(),
            P(),
            P(),
            P(every),
            P(),
            P(BAND + ("x",), "yh"),
        ),
        out_specs=P(BAND + ("x",), "yh"),
        check_vma=False,
    )
```

```python
import math

import jax
import jax.numpy as jnp
import numpy as np
from jax import lax
from jax.experimental import pallas as pl
from jax.experimental.pallas import tpu as pltpu
from jax.sharding import Mesh, PartitionSpec as P

NS = 80
NG = 10240
NCOND = 512
GRID = NS**3
PIECE = 1000
KEPT = 14
BF16 = jnp.bfloat16
F32 = jnp.float32
AXES = ("za", "zb", "yl", "core", "x", "yh")
SIZES = (4, 2, 2, 2, 4, 4)
BAND = ("za", "zb", "yl", "core")
VMEM = pl.BlockSpec(memory_space=pltpu.VMEM)


def tables():
    freq = np.arange(KEPT)
    angle = 2 * np.pi * np.outer(np.arange(NS), freq) / NS
    along_z = np.zeros((NS, 32))
    along_z[:, :KEPT] = np.cos(angle)
    along_z[:, 16 : 16 + KEPT] = np.sin(angle)
    first = np.kron(np.eye(8), along_z)
    core, row = np.divmod(np.arange(800), 400)
    line = 25 * (2 * (row % 16) + core) + row // 16
    angle = 2 * np.pi * np.outer(freq, line // 10) / NS
    along_x = np.zeros((32, 800))
    along_x[:KEPT] = np.cos(angle)
    along_x[16 : 16 + KEPT] = np.sin(angle)
    tens = line % 10
    along_q = np.concatenate(
        [
            np.cos(2 * np.pi * np.outer(np.arange(6), tens) / 10),
            np.sin(2 * np.pi * np.outer(np.arange(1, 5), tens) / 10),
        ]
    )
    second = (along_q[:, None, :] * along_x[None]).reshape(320, 2, 400).transpose(1, 0, 2)
    angle = 2 * np.pi * np.outer(freq, np.arange(256) // 32) / NS
    third = np.zeros((32, 256))
    third[:KEPT] = np.cos(angle)
    third[16 : 16 + KEPT] = np.sin(angle)
    return first, second, third


def segments(m):
    found, lane = [], 0
    while lane < 128:
        piece, inside = divmod(128 * m + lane, PIECE)
        row, start = divmod(inside, 128)
        found.append((piece, row, lane))
        lane += min(128 - lane, 128 - start, PIECE - inside)
    return found


def index_parts(g_index):
    freq_z = g_index % NS
    freq_y = g_index // NS % NS
    freq_x = g_index // (NS * NS)

    def signed(freq):
        return jnp.where(freq > NS // 2, freq - NS, freq)

    x, y, z = signed(freq_x), signed(freq_y), signed(freq_z)
    sign = (x < 0).astype(jnp.int32) + 2 * (y < 0) + 4 * (z < 0)
    high = (jnp.abs(y) // 2) * 16 + jnp.abs(x)
    low = (jnp.abs(y) % 2) * 128 + sign * 16 + jnp.abs(z)
    return low, high


def one_of(values_ref, number):
    match = lax.broadcasted_iota(jnp.int32, values_ref.shape, 1) == number
    return jnp.sum(jnp.where(match, values_ref[...], 0.0), axis=1, keepdims=True)


def widen_kernel(cond_ref, number_ref, out_ref, number_out_ref, wide):
    wide[...] = cond_ref[...].astype(F32).reshape(wide.shape)
    for core in range(2):
        for m in range(125):
            out_ref[core, m] = wide[pl.ds(m + 125 * core, 16, stride=250), :]
    number_out_ref[...] = jnp.broadcast_to(number_ref[...].reshape(1, 1), number_out_ref.shape)


def half_grid(core, valence_ref, cond_ref, first_ref, second_ref, block):
    lane = lax.broadcasted_iota(jnp.int32, (16, 128), 1)
    turned = {}

    def turn(piece, row):
        if (piece, row) not in turned:
            at = 128 * piece + 16 * row
            found = valence_ref[at : at + 16, :].astype(F32)
            shift = 104 * piece % 128
            turned[piece, row] = pltpu.roll(found, shift, 1) if shift else found
        return turned[piece, row]

    parts = []
    for n in range(25):
        for t in range(5):
            m = 5 * n + t
            valence = None
            for piece, row, begin in segments(m):
                found = turn(piece, row)
                valence = found if valence is None else jnp.where(lane >= begin, found, valence)
            block[16 * n : 16 * n + 16, 128 * t : 128 * t + 128] = (valence * cond_ref[core, m]).astype(BF16)
        if n % 5 == 4:
            parts.append(
                jnp.dot(
                    block[16 * (n - 4) : 16 * (n + 1), :],
                    first_ref[...],
                    preferred_element_type=F32,
                ).astype(BF16)
            )
    return jnp.dot(second_ref[core], jnp.concatenate(parts, axis=0), preferred_element_type=F32)


def own_kernel(
    own_ref, cond_ref, first_ref, second_ref, pick_ref, number_ref, val_energy_ref, cond_energy_ref,
    out_ref, weight_ref, block,
):
    core = lax.axis_index("core")
    out_ref[...] = half_grid(core, own_ref, cond_ref, first_ref, second_ref, block)
    e_val = one_of(val_energy_ref, pick_ref[...].reshape(1, 1))
    gap = e_val - one_of(cond_energy_ref, number_ref[0:1, 0:1])
    weight_ref[...] = jnp.broadcast_to(4.0 / (gap * math.sqrt(NCOND)), weight_ref.shape)


def values_kernel(
    weight_ref, half_ref, other_ref, cond_ref, chosen_ref, high_ref, first_ref, second_ref,
    third_ref, out_ref, block, rows, scaled,
):
    weight = weight_ref[0:1, :]
    core = 1 - lax.axis_index("core")
    second = half_ref[...] + half_grid(core, other_ref, cond_ref, first_ref, second_ref, block)

    lane = lax.broadcasted_iota(jnp.int32, (16, 128), 1)
    group = lane // 16
    even = group % 2 == 0
    sx = jnp.where(group & 1 == 0, 1.0, -1.0)
    sy = jnp.where(group & 2 == 0, 1.0, -1.0)
    sz = jnp.where(group & 4 == 0, 1.0, -1.0)
    sxy, sxz, syz = sx * sy, sx * sz, sy * sz
    sxyz = sxy * sz

    def add_lanes(value):
        value = value[:, :128] + value[:, 128:]
        value = value + pltpu.roll(value, 64, 1)
        return value + pltpu.roll(value, 32, 1)

    def split(value):
        other = pltpu.roll(value, 16, 1)
        found = []
        for begin in (0, 16):
            a, b = value[begin : begin + 16], other[begin : begin + 16]
            found += [jnp.where(even, a, b), jnp.where(even, b, a)]
        return found

    planes = []
    for gy in range(KEPT):
        digit, sign = gy % 10, 1.0
        if digit > 5:
            digit, sign = 10 - digit, -1.0
        cosine, sine = third_ref[gy : gy + 1, :], third_ref[16 + gy : 17 + gy, :]
        even_q = second[32 * digit : 32 * digit + 32]
        re, im = even_q * cosine, even_q * sine
        if 1 <= digit <= 4:
            odd_q = second[32 * (digit + 5) : 32 * (digit + 5) + 32]
            re, im = re - (sign * sine) * odd_q, im + (sign * cosine) * odd_q
        ccc, ccs, scc, scs = split(add_lanes(re))
        csc, css, ssc, sss = split(add_lanes(im))
        total = (
            (ccc - syz * css) + (sz * ccs + sy * csc) + (sx * scc - sxz * scs) - (sxy * ssc + sxyz * sss)
        )
        planes.append((total * (1.0 / math.sqrt(GRID))).astype(BF16))
    cube = jnp.concatenate(
        [jnp.concatenate(planes[2 * i : 2 * i + 2], axis=1) for i in range(7)], axis=0
    )

    width = 1280
    place = lax.broadcasted_iota(jnp.int32, (112, width), 0)
    for c in range(NG // width):
        part = slice(c * width, (c + 1) * width)
        found = jnp.dot(cube, chosen_ref[:, part], preferred_element_type=F32)
        found = jnp.sum(jnp.where(place == high_ref[:, part], found, 0.0), axis=0, keepdims=True)
        found = found.astype(BF16).astype(F32)
        for k in range(width // 128):
            at = c * (width // 128) + k
            piece = found[:, 128 * k : 128 * k + 128]
            rows[at : at + 1, :] = piece
            scaled[at : at + 1, :] = weight * piece
    for k in range(16):
        yh, za = k // 4, k % 4
        out_ref[k] = jnp.concatenate(
            [rows[20 * yh : 20 * yh + 20, :], scaled[20 * za : 20 * za + 20, :]], axis=0
        ).astype(BF16)


def chosen_kernel(low_ref, out_ref):
    width = 1280
    inner = lax.broadcasted_iota(jnp.int32, (256, width), 0)
    for c in range(NG // width):
        part = slice(c * width, (c + 1) * width)
        out_ref[:, part] = jnp.where(inner == low_ref[:, part], 1.0, 0.0).astype(BF16)


def spread_kernel(own_ref, number_ref, out_ref, wide):
    wide[...] = own_ref[...].astype(F32)
    for m in range(32):
        found = wide[pl.ds(m, 16, stride=32), :].astype(BF16)
        for k in range(4):
            out_ref[k, 16 * m : 16 * m + 16, :] = found


def pack_kernel(h_ref, out_ref, wide, full):
    wide[...] = h_ref[...].reshape(16 * 40, 128).astype(F32)
    for k in range(40):
        full[:, 128 * k : 128 * k + 128] = wide[pl.ds(k, 16, stride=40), :]
    cols = full[:, 0:2560].astype(BF16)
    lane = lax.broadcasted_iota(jnp.int32, (16, 128), 1)
    core = lax.axis_index("core")
    for k in range(16):
        out_ref[k, :, 0:2560] = cols
        pieces = []
        for c in range(2):
            begin = 80 * ((k // 2 % 2) * 16 + (k % 2) * 8 + 4 * c + k // 4 % 4)
            first, shift = 2560 + begin // 128 * 128, begin % 128
            found = full[:, first : first + 128]
            if shift:
                found = pltpu.roll(found, 128 - shift, 1)
                if shift > 48:
                    after = pltpu.roll(full[:, first + 128 : first + 256], 128 - shift, 1)
                    found = jnp.where(lane < 128 - shift, found, after)
            pieces.append(found)
        mine = jnp.where(core == 0, pieces[0], pieces[1])
        theirs = jnp.where(core == 0, pieces[1], pieces[0])
        out_ref[k, :, 2560:2688] = mine.astype(BF16)
        out_ref[k, :, 2688:2816] = theirs.astype(BF16)


def times(left, right):
    return lax.dot_general(left, right, (((0,), (0,)), ((), ())), preferred_element_type=F32)[0:80]


def given_kernel(all_ref, out_ref):
    out_ref[...] = times(all_ref[:, 2688:2816], all_ref[:, 0:2560]).astype(BF16)


def kept_kernel(all_ref, chi_ref, out_ref):
    out_ref[...] = chi_ref[...] + times(all_ref[:, 2560:2688], all_ref[:, 0:2560])


def finish_kernel(kept_ref, taken_ref, out_ref, total, sent):
    copies = []
    for k in range(5):
        part = pl.ds(16 * k, 16)
        total[part, :] = kept_ref[part, :] + taken_ref[part, :].astype(F32)
        copies.append(pltpu.make_async_copy(total.at[part], out_ref.at[part], sent.at[k]))
        copies[-1].start()
    for copy in copies:
        copy.wait()


def call(kernel, out, in_specs, scratch=(), mib=16, flops=0, moved=0, where=VMEM):
    return pl.pallas_call(
        kernel,
        out_shape=out,
        in_specs=in_specs,
        out_specs=jax.tree.map(lambda _: where, out),
        scratch_shapes=scratch,
        compiler_params=pltpu.CompilerParams(vmem_limit_bytes=mib * 2**20),
        cost_estimate=pl.CostEstimate(flops=flops, bytes_accessed=moved, transcendentals=0),
    )


def body(cond_orbitals, val_orbitals, val_index, val_energy, cond_energy, band_list, g_index, chi_old):
    shape = jax.ShapeDtypeStruct
    piece = lax.dynamic_index_in_dim(val_orbitals, val_index[0], 0, keepdims=False)
    piece = jnp.pad(piece, (0, 24)).reshape(1, 8, 128)
    own = lax.all_to_all(
        jnp.broadcast_to(piece, (64, 8, 128)), ("za", "zb", "yl", "yh"), 0, 0, tiled=True
    )
    orbital, number = call(
        widen_kernel,
        (shape((2, 125, 16, 128), F32), shape((8, 128), jnp.int32)),
        [VMEM] * 2,
        [pltpu.VMEM((4000, 128), F32)],
    )(cond_orbitals, band_list)
    low, high = index_parts(g_index)
    own, low, high = lax.optimization_barrier((own, low, high))
    chosen = call(chosen_kernel, shape((256, NG), BF16), [VMEM])(low.reshape(1, NG))
    spread = call(spread_kernel, shape((4, 512, 128), BF16), [VMEM] * 2, [pltpu.VMEM((512, 128), F32)])(own.reshape(512, 128), number)
    own = lax.all_to_all(spread, "x", 0, 0, tiled=True).reshape(2048, 128)
    other = lax.ppermute(own, "core", [(0, 1), (1, 0)])
    first, second, third = tables()
    first, second, third = jnp.asarray(first, BF16), jnp.asarray(second, BF16), jnp.asarray(third, F32)
    grids = [pltpu.VMEM((400, 640), BF16)]
    half, weight = call(own_kernel, (shape((320, 256), F32), shape((8, 128), F32)), [VMEM] * 8, grids)(
        own, orbital, first, second, val_index, number, val_energy.reshape(1, -1),
        cond_energy.reshape(1, -1),
    )
    values = call(
        values_kernel,
        shape((16, 40, 128), BF16),
        [VMEM] * 9,
        grids + [pltpu.VMEM((80, 128), F32)] * 2,
    )(
        weight, half, other, orbital, chosen, high.reshape(1, NG),
        first, second, third,
    )
    gathered = lax.all_to_all(values, ("yh", "za"), 0, 0, tiled=True)
    packed = call(
        pack_kernel,
        shape((16, 16, 2816), BF16),
        [VMEM],
        [pltpu.VMEM((640, 128), F32), pltpu.VMEM((16, 5120), F32)],
    )(gathered)
    panel = lax.all_to_all(packed, ("x", "zb", "yl"), 0, 0, tiled=True).reshape(256, 2816)
    block = shape((80, 2560), F32)
    given = call(given_kernel, shape((80, 2560), BF16), [VMEM])(panel)
    taken = lax.ppermute(given, "core", [(0, 1), (1, 0)])
    kept = call(kept_kernel, block, [VMEM] * 2)(panel, chi_old)
    return call(
        finish_kernel,
        block,
        [VMEM] * 2,
        [pltpu.VMEM((80, 2560), F32), pltpu.SemaphoreType.DMA((5,))],
        where=pl.BlockSpec(memory_space=pl.ANY),
    )(kept, taken)


def solution(mesh):
    fine = Mesh(mesh.devices.reshape(SIZES), AXES)
    every = AXES
    return jax.shard_map(
        body,
        mesh=fine,
        in_specs=(
            P(every, None),
            P(None, every),
            P(),
            P(),
            P(),
            P(every),
            P(),
            P(BAND + ("x",), "yh"),
        ),
        out_specs=P(BAND + ("x",), "yh"),
        check_vma=False,
    )
```

```python
import math

import jax
import jax.numpy as jnp
import numpy as np
from jax import lax
from jax.experimental import pallas as pl
from jax.experimental.pallas import tpu as pltpu
from jax.sharding import Mesh, PartitionSpec as P

NS = 80
NG = 10240
NCOND = 512
GRID = NS**3
PIECE = 1000
KEPT = 14
BF16 = jnp.bfloat16
F32 = jnp.float32
AXES = ("za", "zb", "yl", "core", "x", "yh")
SIZES = (4, 2, 2, 2, 4, 4)
BAND = ("za", "zb", "yl", "core")
VMEM = pl.BlockSpec(memory_space=pltpu.VMEM)


def tables():
    freq = np.arange(KEPT)
    angle = 2 * np.pi * np.outer(np.arange(NS), freq) / NS
    along_z = np.zeros((NS, 32))
    along_z[:, :KEPT] = np.cos(angle)
    along_z[:, 16 : 16 + KEPT] = np.sin(angle)
    first = np.kron(np.eye(8), along_z)
    core, row = np.divmod(np.arange(800), 400)
    line = 25 * (2 * (row % 16) + core) + row // 16
    angle = 2 * np.pi * np.outer(freq, line // 10) / NS
    along_x = np.zeros((32, 800))
    along_x[:KEPT] = np.cos(angle)
    along_x[16 : 16 + KEPT] = np.sin(angle)
    tens = line % 10
    along_q = np.concatenate(
        [
            np.cos(2 * np.pi * np.outer(np.arange(6), tens) / 10),
            np.sin(2 * np.pi * np.outer(np.arange(1, 5), tens) / 10),
        ]
    )
    second = (along_q[:, None, :] * along_x[None]).reshape(320, 2, 400).transpose(1, 0, 2)
    angle = 2 * np.pi * np.outer(freq, np.arange(256) // 32) / NS
    third = np.zeros((32, 256))
    third[:KEPT] = np.cos(angle)
    third[16 : 16 + KEPT] = np.sin(angle)
    return first, second, third


def segments(m):
    found, lane = [], 0
    while lane < 128:
        piece, inside = divmod(128 * m + lane, PIECE)
        row, start = divmod(inside, 128)
        found.append((piece, row, lane))
        lane += min(128 - lane, 128 - start, PIECE - inside)
    return found


def index_parts(g_index):
    freq_z = g_index % NS
    freq_y = g_index // NS % NS
    freq_x = g_index // (NS * NS)

    def signed(freq):
        return jnp.where(freq > NS // 2, freq - NS, freq)

    x, y, z = signed(freq_x), signed(freq_y), signed(freq_z)
    sign = (x < 0).astype(jnp.int32) + 2 * (y < 0) + 4 * (z < 0)
    high = (jnp.abs(y) // 2) * 16 + jnp.abs(x)
    low = (jnp.abs(y) % 2) * 128 + sign * 16 + jnp.abs(z)
    return low, high


def one_of(values_ref, number):
    match = lax.broadcasted_iota(jnp.int32, values_ref.shape, 1) == number
    return jnp.sum(jnp.where(match, values_ref[...], 0.0), axis=1, keepdims=True)


def widen_kernel(cond_ref, number_ref, out_ref, number_out_ref, wide):
    wide[...] = cond_ref[...].astype(F32).reshape(wide.shape)
    for core in range(2):
        for m in range(125):
            out_ref[core, m] = wide[pl.ds(m + 125 * core, 16, stride=250), :]
    number_out_ref[...] = jnp.broadcast_to(number_ref[...].reshape(1, 1), number_out_ref.shape)


def half_grid(core, valence_ref, cond_ref, first_ref, second_ref, block):
    lane = lax.broadcasted_iota(jnp.int32, (16, 128), 1)
    turned = {}

    def turn(piece, row):
        if (piece, row) not in turned:
            at = 128 * piece + 16 * row
            found = valence_ref[at : at + 16, :].astype(F32)
            shift = 104 * piece % 128
            turned[piece, row] = pltpu.roll(found, shift, 1) if shift else found
        return turned[piece, row]

    parts = []
    for n in range(25):
        for t in range(5):
            m = 5 * n + t
            valence = None
            for piece, row, begin in segments(m):
                found = turn(piece, row)
                valence = found if valence is None else jnp.where(lane >= begin, found, valence)
            block[16 * n : 16 * n + 16, 128 * t : 128 * t + 128] = (valence * cond_ref[core, m]).astype(BF16)
        if n % 5 == 4:
            parts.append(
                jnp.dot(
                    block[16 * (n - 4) : 16 * (n + 1), :],
                    first_ref[...],
                    preferred_element_type=F32,
                ).astype(BF16)
            )
    return jnp.dot(second_ref[core], jnp.concatenate(parts, axis=0), preferred_element_type=F32)


def own_kernel(
    own_ref, cond_ref, first_ref, second_ref, pick_ref, number_ref, val_energy_ref, cond_energy_ref,
    out_ref, weight_ref, block,
):
    core = lax.axis_index("core")
    out_ref[...] = half_grid(core, own_ref, cond_ref, first_ref, second_ref, block)
    e_val = one_of(val_energy_ref, pick_ref[...].reshape(1, 1))
    gap = e_val - one_of(cond_energy_ref, number_ref[0:1, 0:1])
    weight_ref[...] = jnp.broadcast_to(4.0 / (gap * math.sqrt(NCOND)), weight_ref.shape)


def values_kernel(
    weight_ref, half_ref, other_ref, cond_ref, chosen_ref, high_ref, first_ref, second_ref,
    third_ref, out_ref, block, rows, scaled,
):
    weight = weight_ref[0:1, :]
    core = 1 - lax.axis_index("core")
    second = half_ref[...] + half_grid(core, other_ref, cond_ref, first_ref, second_ref, block)

    lane = lax.broadcasted_iota(jnp.int32, (16, 128), 1)
    group = lane // 16
    even = group % 2 == 0
    sx = jnp.where(group & 1 == 0, 1.0, -1.0)
    sy = jnp.where(group & 2 == 0, 1.0, -1.0)
    sz = jnp.where(group & 4 == 0, 1.0, -1.0)
    sxy, sxz, syz = sx * sy, sx * sz, sy * sz
    sxyz = sxy * sz

    def add_lanes(value):
        value = value[:, :128] + value[:, 128:]
        value = value + pltpu.roll(value, 64, 1)
        return value + pltpu.roll(value, 32, 1)

    def split(value):
        other = pltpu.roll(value, 16, 1)
        found = []
        for begin in (0, 16):
            a, b = value[begin : begin + 16], other[begin : begin + 16]
            found += [jnp.where(even, a, b), jnp.where(even, b, a)]
        return found

    planes = []
    for gy in range(KEPT):
        digit, sign = gy % 10, 1.0
        if digit > 5:
            digit, sign = 10 - digit, -1.0
        cosine, sine = third_ref[gy : gy + 1, :], third_ref[16 + gy : 17 + gy, :]
        even_q = second[32 * digit : 32 * digit + 32]
        re, im = even_q * cosine, even_q * sine
        if 1 <= digit <= 4:
            odd_q = second[32 * (digit + 5) : 32 * (digit + 5) + 32]
            re, im = re - (sign * sine) * odd_q, im + (sign * cosine) * odd_q
        ccc, ccs, scc, scs = split(add_lanes(re))
        csc, css, ssc, sss = split(add_lanes(im))
        total = (
            (ccc - syz * css) + (sz * ccs + sy * csc) + (sx * scc - sxz * scs) - (sxy * ssc + sxyz * sss)
        )
        planes.append((total * (1.0 / math.sqrt(GRID))).astype(BF16))
    cube = jnp.concatenate(
        [jnp.concatenate(planes[2 * i : 2 * i + 2], axis=1) for i in range(7)], axis=0
    )

    width = 1280
    place = lax.broadcasted_iota(jnp.int32, (112, width), 0)
    for c in range(NG // width):
        part = slice(c * width, (c + 1) * width)
        found = jnp.dot(cube, chosen_ref[:, part], preferred_element_type=F32)
        found = jnp.sum(jnp.where(place == high_ref[:, part], found, 0.0), axis=0, keepdims=True)
        found = found.astype(BF16).astype(F32)
        for k in range(width // 128):
            at = c * (width // 128) + k
            piece = found[:, 128 * k : 128 * k + 128]
            rows[at : at + 1, :] = piece
    scaled[...] = weight * rows[...]
    for k in range(16):
        yh, za = k % 4, k // 4
        out_ref[k] = jnp.concatenate(
            [rows[20 * yh : 20 * yh + 20, :], scaled[20 * za : 20 * za + 20, :]], axis=0
        ).astype(BF16)


def chosen_kernel(low_ref, out_ref):
    width = 1280
    inner = lax.broadcasted_iota(jnp.int32, (256, width), 0)
    for c in range(NG // width):
        part = slice(c * width, (c + 1) * width)
        out_ref[:, part] = jnp.where(inner == low_ref[:, part], 1.0, 0.0).astype(BF16)


def spread_kernel(own_ref, number_ref, out_ref, wide):
    wide[...] = own_ref[...].astype(F32)
    for m in range(32):
        found = wide[pl.ds(m, 16, stride=32), :].astype(BF16)
        for k in range(4):
            out_ref[k, 16 * m : 16 * m + 16, :] = found


def pack_kernel(h_ref, out_ref, wide, full):
    wide[...] = h_ref[...].reshape(16 * 40, 128).astype(F32)
    for k in range(40):
        full[:, 128 * k : 128 * k + 128] = wide[pl.ds(k, 16, stride=40), :]
    cols = full[:, 0:2560].astype(BF16)
    lane = lax.broadcasted_iota(jnp.int32, (16, 128), 1)
    core = lax.axis_index("core")
    for k in range(16):
        out_ref[k, :, 0:2560] = cols
        pieces = []
        for c in range(2):
            begin = 80 * (k % 4 * 8 + 4 * c + k // 4)
            first, shift = 2560 + begin // 128 * 128, begin % 128
            found = full[:, first : first + 128]
            if shift:
                found = pltpu.roll(found, 128 - shift, 1)
                if shift > 48:
                    after = pltpu.roll(full[:, first + 128 : first + 256], 128 - shift, 1)
                    found = jnp.where(lane < 128 - shift, found, after)
            pieces.append(found)
        mine = jnp.where(core == 0, pieces[0], pieces[1])
        theirs = jnp.where(core == 0, pieces[1], pieces[0])
        out_ref[k, :, 2560:2688] = mine.astype(BF16)
        out_ref[k, :, 2688:2816] = theirs.astype(BF16)


def times(left, right):
    return lax.dot_general(left, right, (((0,), (0,)), ((), ())), preferred_element_type=F32)[0:80]


def given_kernel(all_ref, out_ref):
    out_ref[...] = times(all_ref[:, 2688:2816], all_ref[:, 0:2560]).astype(BF16)


def kept_kernel(all_ref, chi_ref, out_ref):
    out_ref[...] = chi_ref[...] + times(all_ref[:, 2560:2688], all_ref[:, 0:2560])


def finish_kernel(kept_ref, taken_ref, out_ref, total, sent):
    copies = []
    for k in range(5):
        part = pl.ds(16 * k, 16)
        total[part, :] = kept_ref[part, :] + taken_ref[part, :].astype(F32)
        copies.append(pltpu.make_async_copy(total.at[part], out_ref.at[part], sent.at[k]))
        copies[-1].start()
    for copy in copies:
        copy.wait()


def call(kernel, out, in_specs, scratch=(), mib=16, flops=0, moved=0, where=VMEM):
    return pl.pallas_call(
        kernel,
        out_shape=out,
        in_specs=in_specs,
        out_specs=jax.tree.map(lambda _: where, out),
        scratch_shapes=scratch,
        compiler_params=pltpu.CompilerParams(vmem_limit_bytes=mib * 2**20),
        cost_estimate=pl.CostEstimate(flops=flops, bytes_accessed=moved, transcendentals=0),
    )


def body(cond_orbitals, val_orbitals, val_index, val_energy, cond_energy, band_list, g_index, chi_old):
    shape = jax.ShapeDtypeStruct
    piece = lax.dynamic_index_in_dim(val_orbitals, val_index[0], 0, keepdims=False)
    piece = jnp.pad(piece, (0, 24)).reshape(1, 8, 128)
    own = lax.all_to_all(
        jnp.broadcast_to(piece, (64, 8, 128)), ("za", "zb", "yl", "yh"), 0, 0, tiled=True
    )
    orbital, number = call(
        widen_kernel,
        (shape((2, 125, 16, 128), F32), shape((8, 128), jnp.int32)),
        [VMEM] * 2,
        [pltpu.VMEM((4000, 128), F32)],
    )(cond_orbitals, band_list)
    low, high = index_parts(g_index)
    own, low, high = lax.optimization_barrier((own, low, high))
    chosen = call(chosen_kernel, shape((256, NG), BF16), [VMEM])(low.reshape(1, NG))
    spread = call(spread_kernel, shape((4, 512, 128), BF16), [VMEM] * 2, [pltpu.VMEM((512, 128), F32)])(own.reshape(512, 128), number)
    own = lax.all_to_all(spread, "x", 0, 0, tiled=True).reshape(2048, 128)
    other = lax.ppermute(own, "core", [(0, 1), (1, 0)])
    first, second, third = tables()
    first, second, third = jnp.asarray(first, BF16), jnp.asarray(second, BF16), jnp.asarray(third, F32)
    grids = [pltpu.VMEM((400, 640), BF16)]
    half, weight = call(own_kernel, (shape((320, 256), F32), shape((8, 128), F32)), [VMEM] * 8, grids)(
        own, orbital, first, second, val_index, number, val_energy.reshape(1, -1),
        cond_energy.reshape(1, -1),
    )
    values = call(
        values_kernel,
        shape((16, 40, 128), BF16),
        [VMEM] * 9,
        grids + [pltpu.VMEM((80, 128), F32)] * 2,
    )(
        weight, half, other, orbital, chosen, high.reshape(1, NG),
        first, second, third,
    )
    gathered = lax.all_to_all(values, ("za", "yh"), 0, 0, tiled=True)
    packed = call(
        pack_kernel,
        shape((16, 16, 2816), BF16),
        [VMEM],
        [pltpu.VMEM((640, 128), F32), pltpu.VMEM((16, 5120), F32)],
    )(gathered)
    panel = lax.all_to_all(packed, ("x", "zb", "yl"), 0, 0, tiled=True).reshape(256, 2816)
    block = shape((80, 2560), F32)
    given = call(given_kernel, shape((80, 2560), BF16), [VMEM])(panel)
    taken = lax.ppermute(given, "core", [(0, 1), (1, 0)])
    kept = call(kept_kernel, block, [VMEM] * 2)(panel, chi_old)
    return call(
        finish_kernel,
        block,
        [VMEM] * 2,
        [pltpu.VMEM((80, 2560), F32), pltpu.SemaphoreType.DMA((5,))],
        where=pl.BlockSpec(memory_space=pl.ANY),
    )(kept, taken)


def solution(mesh):
    fine = Mesh(mesh.devices.reshape(SIZES), AXES)
    every = AXES
    return jax.shard_map(
        body,
        mesh=fine,
        in_specs=(
            P(every, None),
            P(None, every),
            P(),
            P(),
            P(),
            P(every),
            P(),
            P(BAND + ("x",), "yh"),
        ),
        out_specs=P(BAND + ("x",), "yh"),
        check_vma=False,
    )
```
